256 devices in a mesh: cluster: 64 (over z, x_hi, y), species: 2 (over core), owner: 2 (over x_lo).
Axes of the slice: x: 4 (x_hi: 2, x_lo: 2; x = x_hi * 2 + x_lo), y: 4, z: 8, core: 2. Of those that a mesh axis runs over, the one named last changes fastest.
Arguments:
- state: float32 [4, 64, 512, 256], P('species', None, ('cluster', 'owner')), may hold values from -6 to 6
- near_blocks: bfloat16 [9, 256, 256], replicated, as said below
- basis: bfloat16 [256, 48], replicated, may hold values from -0.375 to 0.375
- leaf_tiles: float32 [40, 48, 48], replicated, may hold values from -0.125 to 0.125
- leaf_links: int32 [64, 512, 40], P(None, ('cluster', 'owner')), may hold values 0 or 1
- up_leaf: float32 [64, 8, 48, 48], P(None, 'owner'), may hold values from -0.0390625 to 0.0390625
- up_coarse: float32 [2, 64, 48, 48], replicated, may hold values from -0.625 to 0.625
- coarse_tiles: float32 [3, 64, 4, 48, 48], P(None, 'cluster', None, None, 'owner'), may hold values from -0.25 to 0.25
- coarse_links: int32 [3, 64, 4], P(None, 'cluster'), may hold values 0 or 1
- down_leaf: float32 [64, 8, 48, 48], P(None, 'owner'), may hold values from -0.875 to 0.875
- diffusion: float32 [4], P('species'), may hold values from 0.5 to 3
- speed: float32 [2, 64, 512, 256], P(None, None, ('cluster', 'owner')), may hold values from 0.5 to 4
- upwind: int32 [2, 64, 512, 256], P(None, None, ('cluster', 'owner')), may hold values from 0 to 1
- zone: int32 [64, 512, 256], P(None, ('cluster', 'owner')), may hold values from 0 to 15
- rate: float32 [16, 4, 4], replicated, may hold values from -6 to 6
Outputs:
- new_state: float32 [4, 64, 512, 256], P('species', None, ('cluster', 'owner'))
The draws below stay inside these ranges and needn't reach their ends.
Inputs may be any that keep to these rules, and one draw needn't show every extreme that they name: The diagonal of the centre block near_blocks[4] lies between 1.8 and 6.2.
All inputs are finite; a program needn't handle non-finite values. No bound on the sum of `leaf_links` or of `coarse_links` on one device may be relied on, other than what follows from the above.
Results may differ from the reference program's by a relative error of at most 0.0021.
The reference program's roundings to bfloat16 on the way (of `state_low` and `field_low`) count: a program that leaves them out, or rounds other values in their place, can miss the bound.
Values may be sent and summed in bfloat16 or wider, within the bound.
A program may use at most 128 MiB of HBM per device.

```python
import math
import jax
import jax.numpy as jnp
from jax import lax

SIDE = 16
LEAF = 256
RANK = 48
NS = 4
PY = 64
LEVELS = 3
SWEEPS = 2
ZONES = 16
NCL = 64
PXC = 8
PXT = 512


def draw_near_blocks(key, part):
    key = jax.random.fold_in(key, 11)
    key_spread, key_centre = jax.random.split(key)
    spread = 0.02 * jax.random.normal(key_spread, (9, LEAF, LEAF), jnp.float32)
    centre = jnp.exp(jax.random.uniform(key_centre, (LEAF,), jnp.float32, jnp.log(2.0), jnp.log(6.0)))
    spread = spread.at[4].add(jnp.diag(centre))
    return spread.astype(jnp.bfloat16)


def set_ends(array, key, smallest, top_value):
    spot = [jax.random.randint(jax.random.fold_in(key, axis), (), 0, length) for axis, length in enumerate(array.shape)]
    main_axis = array.shape.index(max(array.shape))
    next_to = spot[:main_axis] + [(spot[main_axis] + 1) % array.shape[main_axis]] + spot[main_axis + 1:]
    return array.at[tuple(spot)].set(smallest).at[tuple(next_to)].set(top_value)


def level_of(rng, extent, shards, least, high):
    def one(dim, parts):
        draws = jax.random.uniform(jax.random.fold_in(jax.random.fold_in(rng, 6), dim), (parts,), jnp.float32, least / len(shards), high / len(shards))
        return jnp.repeat(jnp.exp(draws), extent[dim] // parts).reshape((-1,) + (1,) * (len(extent) - dim - 1))

    level = one(*shards[0])
    for cut in shards[1:]:
        level = level * one(*cut)
    return level


def scatter_about(rng, dims, scale, bound, pieces=(), kind=jnp.bfloat16):
    gain = level_of(rng, dims, pieces, -0.22, 0.18) if pieces else 1.0
    entries = jax.random.normal(rng, dims, jnp.float32) * scale * gain
    return jnp.minimum(jnp.maximum(entries, -bound), bound).astype(kind)


def setup_inputs(seed: int = 0) -> dict:
    arg_keys = jax.random.split(jax.random.key(seed), 16)
    return {
        "state": scatter_about(arg_keys[0], (NS, PY, PXT, LEAF), 1.0, 6.0, ((0, 2), (2, 128)), jnp.float32),
        "near_blocks": draw_near_blocks(jax.random.fold_in(arg_keys[15], 71), 0),
        "basis": scatter_about(arg_keys[2], (LEAF, RANK), LEAF ** -0.5, 0.375),
        "leaf_tiles": scatter_about(arg_keys[3], (40, RANK, RANK), (40 * RANK) ** -0.5, 0.125, (), jnp.float32),
        "leaf_links": set_ends((jax.random.randint(arg_keys[4], (PY, PXT, 40), 0, 4) < 3).astype(jnp.int32), jax.random.fold_in(arg_keys[4], 1), 0, 1),
        "up_leaf": scatter_about(arg_keys[5], (PY, PXC, RANK, RANK), (PY * PXC * RANK) ** -0.5, 0.0390625, ((1, 2),), jnp.float32),
        "up_coarse": scatter_about(arg_keys[6], (LEVELS - 1, NCL, RANK, RANK), (2 * RANK) ** -0.5, 0.625, (), jnp.float32),
        "coarse_tiles": scatter_about(arg_keys[7], (LEVELS, NCL, 4, RANK, RANK), (4 * LEVELS * RANK) ** -0.5, 0.25, ((1, 64), (4, 2)), jnp.float32),
        "coarse_links": set_ends((jax.random.randint(arg_keys[8], (LEVELS, NCL, 4), 0, 4) < 3).astype(jnp.int32), jax.random.fold_in(arg_keys[8], 1), 0, 1),
        "down_leaf": scatter_about(arg_keys[9], (PY, PXC, RANK, RANK), RANK ** -0.5, 0.875, ((1, 2),), jnp.float32),
        "diffusion": jnp.clip(jnp.exp(math.log(3.0) - 1.7917595 * jax.random.uniform(arg_keys[10], (NS,), jnp.float32) ** level_of(arg_keys[10], (NS,), ((0, 2),), -0.2, 0.2)), 0.5, 3.0),
        "speed": jnp.clip(jnp.exp(math.log(4.0) - 2.0794415 * jax.random.uniform(arg_keys[11], (2, PY, PXT, LEAF), jnp.float32) ** level_of(arg_keys[11], (2, PY, PXT, LEAF), ((2, 128),), -0.2, 0.2)), 0.5, 4.0),
        "upwind": set_ends(jax.random.randint(arg_keys[12], (2, PY, PXT, LEAF), 0, 2), jax.random.fold_in(arg_keys[12], 1), 0, 1).astype(jnp.int32),
        "zone": set_ends(jax.random.randint(arg_keys[13], (PY, PXT, LEAF), 0, ZONES), jax.random.fold_in(arg_keys[13], 1), 0, ZONES - 1).astype(jnp.int32),
        "rate": scatter_about(arg_keys[14], (ZONES, NS, NS), 1.5, 6.0, (), jnp.float32),
    }


time_step = 0.1
exact_result = lax.Precision.HIGHEST
near_offsets = [(y_step, x_step) for y_step in (-1, 0, 1) for x_step in (-1, 0, 1)]
far_offsets = [(y_step, x_step) for y_step in range(-3, 4) for x_step in range(-3, 4) if max(abs(y_step), abs(x_step)) >= 2]
group_offsets = [2, 3, -2, -3]


def patches_to_grid(values, patch_side):
    lead_dims = values.shape[:-3]
    row_count, col_count = values.shape[-3], values.shape[-2]
    count_lead = len(lead_dims)
    shaped = values.reshape(lead_dims + (row_count, col_count, patch_side, patch_side))
    ordering = tuple(range(count_lead)) + (count_lead, count_lead + 2, count_lead + 1, count_lead + 3)
    return jnp.transpose(shaped, ordering).reshape(lead_dims + (row_count * patch_side, col_count * patch_side))


def grid_to_patches(values, patch_side):
    lead_dims = values.shape[:-2]
    row_count = values.shape[-2] // patch_side
    col_count = values.shape[-1] // patch_side
    count_lead = len(lead_dims)
    shaped = values.reshape(lead_dims + (row_count, patch_side, col_count, patch_side))
    ordering = tuple(range(count_lead)) + (count_lead, count_lead + 2, count_lead + 1, count_lead + 3)
    return jnp.transpose(shaped, ordering).reshape(lead_dims + (row_count, col_count, patch_side * patch_side))


def advect(state_low, speed, upwind):
    values = patches_to_grid(state_low.astype(jnp.float32), SIDE)
    speed_grid = patches_to_grid(speed, SIDE)
    upwind_grid = patches_to_grid(upwind, SIDE)
    flux_x = jnp.where(upwind_grid[0] == 0, speed_grid[0] * jnp.roll(values, 1, axis=2), -speed_grid[0] * values)
    flux_y = jnp.where(upwind_grid[1] == 0, speed_grid[1] * jnp.roll(values, 1, axis=1), -speed_grid[1] * values)
    change = flux_x - jnp.roll(flux_x, -1, axis=2) + flux_y - jnp.roll(flux_y, -1, axis=1)
    return grid_to_patches(change, SIDE)


def react(state, rate, zone):
    hyperbolic_values = jnp.tanh(state)
    total = jnp.zeros(state.shape, jnp.float32)
    for zone_idx in range(ZONES):
        contrib = jnp.einsum("st,tyxn->syxn", rate[zone_idx], hyperbolic_values, precision=exact_result)
        total = total + jnp.where(zone[None] == zone_idx, contrib, 0.0)
    return total


def apply_operator(state_low, near_blocks, basis, leaf_tiles, leaf_links, up_leaf, up_coarse, coarse_tiles, coarse_links, down_leaf):
    species = state_low.shape[0]
    near_part = jnp.zeros(state_low.shape, jnp.float32)
    for index_near, (y_step, x_step) in enumerate(near_offsets):
        shifted = jnp.roll(jnp.roll(state_low, -y_step, axis=1), -x_step, axis=2)
        product_term = jnp.dot(shifted.reshape(-1, LEAF), near_blocks[index_near], preferred_element_type=jnp.float32)
        near_part = near_part + product_term.reshape(state_low.shape)
    expansion_terms = jnp.dot(state_low.reshape(-1, LEAF), basis, preferred_element_type=jnp.float32)
    expansion_terms = expansion_terms.reshape(species, PY, PXT, RANK)
    local_field = jnp.zeros(expansion_terms.shape, jnp.float32)
    for index_far, (y_step, x_step) in enumerate(far_offsets):
        shifted = jnp.roll(jnp.roll(expansion_terms, -y_step, axis=1), -x_step, axis=2)
        product_term = jnp.einsum("syxr,rq->syxq", shifted, leaf_tiles[index_far], precision=exact_result)
        link_mask = leaf_links[:, :, index_far].astype(jnp.float32)[None, :, :, None]
        local_field = local_field + link_mask * product_term
    by_cluster = expansion_terms.reshape(species, PY, NCL, PXC, RANK)
    values_by_level = jnp.einsum("sycpr,yprq->csq", by_cluster, up_leaf, precision=exact_result)
    coarse = jnp.zeros((NCL, species, RANK), jnp.float32)
    cluster_ids = jnp.arange(NCL).astype(jnp.int32)
    for level_idx in range(LEVELS):
        groups = NCL >> level_idx
        if level_idx > 0:
            paired = values_by_level.reshape(groups, 2, species, RANK)
            transfer = up_coarse[level_idx - 1, :2 * groups].reshape(groups, 2, RANK, RANK)
            values_by_level = jnp.einsum("gcsr,gcrq->gsq", paired, transfer, precision=exact_result)
        for index_group, offset in enumerate(group_offsets):
            partner = ((cluster_ids // (2 ** level_idx) + offset) % groups).astype(jnp.int32)
            gathered = values_by_level[partner]
            product_term = jnp.einsum("dsr,drq->dsq", gathered, coarse_tiles[level_idx, :, index_group], precision=exact_result)
            link_mask = coarse_links[level_idx, :, index_group].astype(jnp.float32)[:, None, None]
            coarse = coarse + link_mask * product_term
    expanded = jnp.einsum("csr,yprq->sycpq", coarse, down_leaf, precision=exact_result).reshape(species, PY, PXT, RANK)
    field_low = (local_field + expanded).astype(jnp.bfloat16)
    far_part = jnp.dot(field_low.reshape(-1, RANK), basis.T, preferred_element_type=jnp.float32)
    return near_part + far_part.reshape(state_low.shape)


def reference(state, near_blocks, basis, leaf_tiles, leaf_links, up_leaf, up_coarse, coarse_tiles, coarse_links, down_leaf, diffusion, speed, upwind, zone, rate):
    state_low = state.astype(jnp.bfloat16)
    explicit = advect(state_low, speed, upwind) + react(state, rate, zone)
    target = state + time_step * explicit
    centre = jnp.diagonal(near_blocks[4]).astype(jnp.float32)
    scaled = time_step * diffusion[:, None, None, None]
    inverse_diag = 1.0 / (1.0 + scaled * centre)
    current_guess = state
    for sweep_idx in range(SWEEPS):
        applied = apply_operator(current_guess.astype(jnp.bfloat16), near_blocks, basis, leaf_tiles, leaf_links, up_leaf, up_coarse, coarse_tiles, coarse_links, down_leaf)
        current_guess = current_guess + (target - current_guess - scaled * applied) * inverse_diag
    return current_guess
```

```python
import jax
import jax.numpy as jnp
from jax import lax
from jax.experimental import pallas as pl
from jax.experimental.pallas import tpu as pltpu
from jax.sharding import PartitionSpec as P

F32 = jnp.float32
BF16 = jnp.bfloat16
I32 = jnp.int32
SWEEPS = 2
STEP = 0.1
RANK = 48
PY = 64
HIGHEST = lax.Precision.HIGHEST
NT = (((1,), (1,)), ((), ()))
TN = (((0,), (0,)), ((), ()))
NN = (((1,), (0,)), ((), ()))
FAR = [(dy, dx) for dy in range(-3, 4) for dx in range(-3, 4) if max(abs(dy), abs(dx)) >= 2]
GROUP_OFFSETS = (2, 3, -2, -3)
REACH = (-3, -2, -1, 1, 2, 3)


def dot(a, b, dims, precision=None):
    return lax.dot_general(a, b, dims, precision=precision, preferred_element_type=F32)


def lanes(shape):
    return lax.broadcasted_iota(I32, shape, len(shape) - 1)


def rows(shape):
    return lax.broadcasted_iota(I32, shape, len(shape) - 2)


def shift_rows_in_lanes(x, dy):
    if dy == 0:
        return x
    near = pltpu.roll(x, (-dy) % 128, 1)
    wrapped = pltpu.roll(x, (64 - dy) % 128, 1)
    at = lanes(x.shape) % 64 + dy
    return jnp.where((at >= 0) & (at < 64), near, wrapped)


def row_products(total, a_ref, w_ref, px):
    def block(i, acc):
        first = pl.multiple_of(i * 8, 8)
        a = a_ref[pl.ds(first, 8), :]
        for j in range(8):
            acc = acc + a[j : j + 1, :] * w_ref[px, first + j]
        return acc

    return lax.fori_loop(0, RANK // 8, block, total)


def kernel(
    state, near_blocks, basis_t, leaf_tiles, links, up_leaf, down_leaf, up_coarse, tiles, speed, upwind, zone,
    rate, coarse_links, diffusion,
    out,
    s0, cur, tgt, near_acc, low, oth, ctf, ctb, ctx, q, spd, upw, zon, nb, bt, lt, ltt, lk, msk, rhs,
    u_raw, u_dup, d_raw, d_dup, upc, upg, tcx, t2, tab, level, cfb, expd, p1, r2,
    load_sem, load8_sem, p1_send, p1_recv, r2_send, r2_recv, halo_send, halo_recv, one_send, one_recv,
):
    cluster = lax.axis_index("cluster")
    owner = lax.axis_index("owner")
    species = lax.axis_index("species")
    n_clusters = lax.axis_size("cluster")
    group = cluster // 4
    y0 = cluster % 4
    n_groups = n_clusters // 4
    slot = y0 * 2 + owner
    line = cluster * 2 + owner
    n_line = n_clusters * 2
    right = lax.rem(line + 1, n_line)
    left = lax.rem(line + n_line - 1, n_line)
    right_id = {"cluster": right // 2, "owner": right % 2}
    left_id = {"cluster": left // 2, "owner": left % 2}
    other_id = {"species": 1 - species}

    def ring_id(k):
        there = lax.rem(slot + k, 8)
        return {"cluster": group * 4 + there // 2, "owner": there % 2}

    def reach_id(d):
        return {"cluster": lax.rem(group + d + n_groups, n_groups) * 4 + y0}

    def load(src, dst, i):
        copy = pltpu.make_async_copy(src, dst, load_sem.at[i])
        copy.start()
        return copy

    state_loads = []
    for s in range(2):
        for px in range(4):
            copy = pltpu.make_async_copy(state.at[s, :, px], s0.at[px, pl.ds(64 * s, 64)], load8_sem.at[0, s * 4 + px])
            copy.start()
            state_loads.append(copy)
    bt_load = load(basis_t, bt, 0)
    flow_loads = []
    for j, (src, dst) in enumerate(((speed, spd), (upwind, upw))):
        for e in range(2):
            for px in range(4):
                copy = pltpu.make_async_copy(src.at[e, :, px], dst.at[e, px], load8_sem.at[1 + j, e * 4 + px])
                copy.start()
                flow_loads.append(copy)
    u_loads = [load(up_leaf.at[px], u_raw.at[px], 1 + px) for px in range(4)]
    tiles_load = load(tiles, tcx.at[:, :, owner], 5)
    zone_loads = []
    for px in range(4):
        copy = pltpu.make_async_copy(zone.at[:, px], zon.at[px], load8_sem.at[3, px])
        copy.start()
        zone_loads.append(copy)
    nb_load = load(near_blocks, nb, 6)
    lk_load = load(links, lk, 7)
    upc_load = load(up_coarse, upc, 8)
    lt_load = load(leaf_tiles, lt, 9)
    d_loads = [load(down_leaf.at[px], d_raw.at[px], 10 + px) for px in range(4)]

    r2[:, 7:] = jnp.zeros((SWEEPS, 9, 8, 128), F32)
    barrier = pltpu.get_barrier_semaphore()
    partners = [ring_id(k) for k in range(1, 8)] + [reach_id(d) for d in REACH] + [left_id, right_id, other_id]
    for partner in partners:
        pl.semaphore_signal(barrier, inc=1, device_id=partner, device_id_type=pl.DeviceIdType.MESH)

    def remote(src, dst, send, recv, device_id):
        return pltpu.make_async_remote_copy(
            src_ref=src, dst_ref=dst, send_sem=send, recv_sem=recv,
            device_id=device_id, device_id_type=pl.DeviceIdType.MESH,
        )

    scale_0 = STEP * diffusion[0]
    scale_1 = STEP * diffusion[1]
    scale = jnp.where(lax.broadcasted_iota(I32, (128, 1), 0) < 64, scale_0, scale_1)

    tab[...] = jnp.zeros_like(tab)

    def own_columns(k, src):
        def column(px, _):
            v = src[px].astype(BF16)
            low[k, px + 1] = v
            coeffs = dot(bt[...], v, NT)
            ctf[px] = coeffs
            ctb[k, px + 3] = coeffs.astype(BF16)
            return 0

        lax.fori_loop(0, 4, column, 0)

    def halo_copies(k):
        h, g = halo_send, halo_recv
        return [
            remote(low.at[k, 4], low.at[k, 0], h.at[k, 0], g.at[k, 0], right_id),
            remote(low.at[k, 1], low.at[k, 5], h.at[k, 1], g.at[k, 1], left_id),
            remote(ctb.at[k, pl.ds(4, 3)], ctb.at[k, pl.ds(0, 3)], h.at[k, 2], g.at[k, 2], right_id),
            remote(ctb.at[k, pl.ds(3, 3)], ctb.at[k, pl.ds(7, 3)], h.at[k, 3], g.at[k, 3], left_id),
        ]

    def root_tile(total):
        pick_row = rows((8, 128)) - 2 * y0
        pick = jnp.where((pick_row >= 0) & (pick_row < 2) & (lanes((8, 128)) // 64 == pick_row), 1.0, 0.0)
        padded = jnp.concatenate([total, jnp.zeros((128 - RANK, 128), F32)], axis=0)
        return dot(pick, padded, NT, HIGHEST)

    def send_roots(k, total):
        p1[k, 0] = root_tile(total)
        copies = [remote(p1.at[k, 0], p1.at[k, j], p1_send.at[k, j], p1_recv.at[k, j], ring_id(j)) for j in range(1, 8)]
        for copy in copies:
            copy.start()
        return copies

    def send_groups(k, copies):
        for copy in copies:
            copy.wait_recv()
        tile = p1[k, 0]
        for j in range(1, 8):
            tile = tile + p1[k, j]
        r2[k, 3] = tile
        sends = [
            remote(r2.at[k, 3], r2.at[k, 3 - d], r2_send.at[k, 3 + d], r2_recv.at[k, 3 + d], reach_id(d)) for d in REACH
        ]
        for copy in sends:
            copy.start()
        return sends

    def near(k):
        for dy in (0, -1, 1):
            wide = jnp.concatenate([low[k, dx + 1 : dx + 5].reshape(512, 256) for dx in (-1, 0, 1)], axis=1)
            at = 3 * (dy + 1)
            part = dot(wide, nb[at : at + 3].reshape(768, 256), NN)
            for b in range(8):
                block = part[64 * b : 64 * b + 64]
                px, s = b // 2, b % 2
                if dy == 0:
                    near_acc[px, pl.ds(64 * s, 64)] = block
                else:
                    near_acc[px, pl.ds(64 * s, 64)] += pltpu.roll(block, (-dy) % 64, 0)

    def leaf(k):
        def widen(px, _):
            ctx[px] = ctb[k, px].astype(F32)
            return 0

        lax.fori_loop(0, 10, widen, 0)
        first = 0
        for dy in range(-3, 4):
            mine = [dx for y, dx in FAR if y == dy]
            n = len(mine)

            def stack(px, _, mine=mine, first=first):
                for i, dx in enumerate(mine):
                    masked = ctx[px + 3 + dx] * msk[px, first + i : first + i + 1, :]
                    rhs[px, pl.ds(i * RANK, RANK), :] = masked.astype(BF16)
                return 0

            lax.fori_loop(0, 4, stack, 0)
            for px in range(4):
                part = dot(ltt[:, first * RANK : (first + n) * RANK], rhs[px, : n * RANK, :], NN)
                part = shift_rows_in_lanes(part, dy)
                if first == 0:
                    expd[px] = part
                else:
                    expd[px] += part
            first += n

    def prepare_masks():
        for px in range(4):
            both = jnp.concatenate([lk[px].astype(F32)] * 2, axis=1)
            first = 0
            for dy in range(-3, 4):
                n = sum(1 for y, _ in FAR if y == dy)
                msk[px, first : first + n, :] = shift_rows_in_lanes(both[first : first + n], -dy)
                first += n

    def prepare_leaf_tiles():
        first = 0
        for dy in range(-3, 4):
            n = sum(1 for y, _ in FAR if y == dy)
            stacked = lt[first : first + n].reshape(n * RANK, RANK)
            ltt[:, first * RANK : (first + n) * RANK] = jnp.swapaxes(stacked, 0, 1).astype(BF16)
            first += n

    def prepare_coarse():
        lane = lanes((64, 128))
        at_group = group + lane // 8 - 3 + n_groups
        at_y = (lane // 2) % 4
        for i, target in enumerate(((4 * at_group + at_y) % n_clusters, (2 * at_group + at_y // 2) % (n_clusters // 2))):
            pick = jnp.where((rows((64, 128)) == target) & (lane < 56), 1.0, 0.0).astype(BF16)

            def block(b, _, pick=pick, i=i):
                x = upc[i, pl.ds(b * 8, 8)].reshape(8 * RANK, 64)
                high = x.astype(BF16)
                rest = (x - high.astype(F32)).astype(BF16)
                upg[i, pl.ds(b * 8, 8)] = (dot(high, pick, NN) + dot(rest, pick, NN)).reshape(8, RANK, 128)
                return 0

            lax.fori_loop(0, RANK // 8, block, 0)
        for l in range(3):
            for k in range(4):
                at = (l * 4 + k) * RANK
                t2[:, at : at + RANK] = tcx[l, k].reshape(RANK, RANK)

    def coarse(k):
        zero = jnp.zeros((RANK, 128), F32)
        lane = lanes((1, 128))
        at_d, at_y = lane // 8 - 3, (lane // 2) % 4
        wide_lane = lanes((RANK, 128))
        values = jnp.swapaxes(r2[k].reshape(128, 128), 0, 1)[:RANK]
        pieces = []
        for l in range(3):
            if l > 0:
                level[...] = values
                raised = row_products(zero, level, upg, l - 1)
                hop = 2 * l
                sibling = jnp.where((wide_lane // hop) % 2 == 0, pltpu.roll(raised, 128 - hop, 1), pltpu.roll(raised, hop, 1))
                values = raised + sibling
            for i, offset in enumerate(GROUP_OFFSETS):
                if l == 0:
                    hit = at_d * 4 + at_y == y0 + offset
                elif l == 1:
                    hit = (at_d * 2 + at_y // 2 == y0 // 2 + offset) & (at_y % 2 == 0)
                else:
                    hit = (at_d == offset) & (at_y == 0)
                hit = hit & (lane < 56)
                pieces.append(values * jnp.where(hit, coarse_links[l, 0, i].astype(F32), 0.0))
        found = dot(t2[...], jnp.concatenate(pieces, axis=0), NN, HIGHEST)
        spread = jnp.where(rows((128, 128)) % 2 == lanes((128, 128)) // 64, 1.0, 0.0)
        cfb[...] = dot(found, spread, NN, HIGHEST)

    def finish(k, src, dst, inverse_diag):
        def column(px, _):
            field = row_products(expd[px], cfb, d_dup, px).astype(BF16)
            applied = near_acc[px] + dot(field, bt[...], TN)
            v = src[px]
            dst[px] = v + (tgt[px] - v - scale * applied) * inverse_diag
            return 0

        lax.fori_loop(0, 4, column, 0)

    def reaction(px, _):
        z = zon[px]
        values = [jnp.tanh(s0[px, :64]), jnp.tanh(s0[px, 64:])]
        there = oth[px].astype(F32)
        values += [jnp.tanh(there[:64]), jnp.tanh(there[64:])]
        for s in range(2):
            total = jnp.zeros((64, 256), F32)
            for t in range(4):
                table = jnp.broadcast_to(tab[4 * s + t : 4 * s + t + 1, :], (64, 128))
                found = [jnp.take_along_axis(table, z[:, h : h + 128], axis=1) for h in (0, 128)]
                total = total + jnp.concatenate(found, axis=1) * values[t]
            tgt[px, pl.ds(64 * s, 64)] = s0[px, pl.ds(64 * s, 64)] + STEP * total
        return 0

    def advection(s, _):
        at = pl.ds(pl.multiple_of(s * 64, 64), 64)
        n = lanes((64, 256))

        def flux_x(px):
            v = low[0, px + 1, at].astype(F32)
            before = low[0, px, at].astype(F32)
            v_left = pltpu.roll(jnp.where(n % 16 == 15, pltpu.roll(before, 256 - 16, 1), v), 1, 1)
            w = q[0, px]
            return v, w * jnp.where(w > 0, v_left, v)

        v, flux = flux_x(0)
        for px in range(4):
            v_next, flux_next = flux_x(px + 1)
            flux_right = pltpu.roll(jnp.where(n % 16 == 0, pltpu.roll(flux_next, 16, 1), flux), 255, 1)
            v_up = pltpu.roll(jnp.where(n >= 240, pltpu.roll(v, 1, 0), v), 16, 1)
            w = q[1, px]
            flux_y = w * jnp.where(w > 0, v_up, v)
            flux_down = pltpu.roll(jnp.where(n < 16, pltpu.roll(flux_y, 63, 0), flux_y), 256 - 16, 1)
            tgt[px, at] += STEP * (flux - flux_right + flux_y - flux_down)
            v, flux = v_next, flux_next
        return 0

    for copy in state_loads:
        copy.wait()
    bt_load.wait()
    own_columns(0, s0)
    pl.semaphore_wait(barrier, len(partners))
    halos = halo_copies(0)
    others = remote(low.at[0, pl.ds(1, 4)], oth, one_send.at[0], one_recv.at[0], other_id)
    for copy in halos:
        copy.start()
    others.start()
    tiles_load.wait()
    tile_copy = remote(tcx.at[:, :, owner], tcx.at[:, :, owner], one_send.at[1], one_recv.at[1], {"owner": 1 - owner})
    tile_copy.start()
    for copy in flow_loads:
        copy.wait()

    def signed(px, _):
        for e in range(2):
            v = spd[e, px]
            q[e, px] = jnp.where(upw[e, px] == 0, v, -v)
        return 0

    lax.fori_loop(0, 4, signed, 0)
    edge = remote(q.at[0, 0], q.at[0, 4], one_send.at[2], one_recv.at[2], left_id)
    edge.start()

    for copy in u_loads:
        copy.wait()

    def doubled(raw, dup):
        def block(i, _):
            x = raw[i // RANK, i % RANK]
            dup[i // RANK, i % RANK] = jnp.concatenate([x, x], axis=1)
            return 0

        lax.fori_loop(0, 4 * RANK, block, 0, unroll=8)

    doubled(u_raw, u_dup)

    def roots():
        total = jnp.zeros((RANK, 128), F32)
        for px in range(4):
            total = row_products(total, ctf.at[px], u_dup, px)
        return total

    ring = send_roots(0, roots())

    for s in range(2):
        for t in range(4):
            at = (2 * species + t) % 4
            tab[4 * s + t : 4 * s + t + 1, :16] = rate[2 * species + s, pl.ds(at, 1), :]
    for copy in zone_loads:
        copy.wait()
    others.wait_recv()
    lax.fori_loop(0, 4, reaction, 0)

    reach = send_groups(0, ring)
    for copy in halos:
        copy.wait_recv()
    edge.wait_recv()
    lax.fori_loop(0, 2, advection, 0)
    nb_load.wait()
    near(0)
    eye = rows((256, 256)) == lanes((256, 256))
    diag = jnp.sum(jnp.where(eye, nb[4].astype(F32), 0.0), axis=0, keepdims=True)
    inverse_diag = 1.0 / (1.0 + scale * diag)
    lk_load.wait()
    prepare_masks()
    lt_load.wait()
    prepare_leaf_tiles()
    leaf(0)
    upc_load.wait()
    tile_copy.wait_recv()
    prepare_coarse()
    for copy in d_loads:
        copy.wait()
    doubled(d_raw, d_dup)
    for copy in reach:
        copy.wait_recv()
    coarse(0)
    finish(0, s0, cur, inverse_diag)

    own_columns(1, cur)
    halos_1 = halo_copies(1)
    for copy in halos_1:
        copy.start()
    ring_1 = send_roots(1, roots())
    for copy in halos_1:
        copy.wait_recv()
    near(1)
    reach_1 = send_groups(1, ring_1)
    leaf(1)
    for copy in reach_1:
        copy.wait_recv()
    coarse(1)
    finish(1, cur, out, inverse_diag)

    for copy in halos + halos_1 + [others, tile_copy, edge] + ring + ring_1 + reach + reach_1:
        copy.wait_send()


def per_device(
    state, near_blocks, basis, leaf_tiles, leaf_links, up_leaf, up_coarse, coarse_tiles, coarse_links,
    down_leaf, diffusion, speed, upwind, zone, rate,
):
    anywhere = pl.BlockSpec(memory_space=pl.ANY)
    vmem = pl.BlockSpec(memory_space=pltpu.VMEM)
    smem = pl.BlockSpec(memory_space=pltpu.SMEM)
    dma = pltpu.SemaphoreType.DMA
    scratch = [
        pltpu.VMEM((4, 128, 256), F32),
        pltpu.VMEM((4, 128, 256), F32),
        pltpu.VMEM((4, 128, 256), F32),
        pltpu.VMEM((4, 128, 256), F32),
        pltpu.VMEM((2, 6, 128, 256), BF16),
        pltpu.VMEM((4, 128, 256), BF16),
        pltpu.VMEM((4, RANK, 128), F32),
        pltpu.VMEM((2, 10, RANK, 128), BF16),
        pltpu.VMEM((10, RANK, 128), F32),
        pltpu.VMEM((2, 5, 64, 256), F32),
        pltpu.VMEM((2, 4, 64, 256), F32),
        pltpu.VMEM((2, 4, 64, 256), I32),
        pltpu.VMEM((4, 64, 256), I32),
        pltpu.VMEM((9, 256, 256), BF16),
        pltpu.VMEM((RANK, 256), BF16),
        pltpu.VMEM((40, RANK, RANK), F32),
        pltpu.VMEM((RANK, 40 * RANK), BF16),
        pltpu.VMEM((4, 40, 64), I32),
        pltpu.VMEM((4, 40, 128), F32),
        pltpu.VMEM((4, 7 * RANK, 128), BF16),
        pltpu.VMEM((4, RANK, RANK, 64), F32),
        pltpu.VMEM((4, RANK, RANK, 128), F32),
        pltpu.VMEM((4, RANK, RANK, 64), F32),
        pltpu.VMEM((4, RANK, RANK, 128), F32),
        pltpu.VMEM((2, RANK, RANK, 64), F32),
        pltpu.VMEM((2, RANK, RANK, 128), F32),
        pltpu.VMEM((3, 4, 2, 24, RANK), F32),
        pltpu.VMEM((RANK, 12 * RANK), F32),
        pltpu.VMEM((8, 128), F32),
        pltpu.VMEM((RANK, 128), F32),
        pltpu.VMEM((RANK, 128), F32),
        pltpu.VMEM((4, RANK, 128), F32),
        pltpu.VMEM((2, 8, 8, 128), F32),
        pltpu.VMEM((2, 16, 8, 128), F32),
        dma((14,)),
        dma((4, 8)),
        dma((2, 8)),
        dma((2, 8)),
        dma((2, 7)),
        dma((2, 7)),
        dma((2, 4)),
        dma((2, 4)),
        dma((3,)),
        dma((3,)),
    ]
    result = pl.pallas_call(
        kernel,
        out_shape=jax.ShapeDtypeStruct((4, 128, 256), F32),
        in_specs=[anywhere] * 12 + [vmem, smem, smem],
        out_specs=vmem,
        scratch_shapes=scratch,
        compiler_params=pltpu.CompilerParams(
            collective_id=0, has_side_effects=True, vmem_limit_bytes=56 * 1024 * 1024
        ),
    )(
        state,
        near_blocks,
        basis.T,
        leaf_tiles,
        jnp.transpose(leaf_links, (1, 2, 0)),
        jnp.transpose(up_leaf, (1, 2, 3, 0)),
        jnp.transpose(down_leaf, (1, 2, 3, 0)),
        jnp.transpose(up_coarse, (0, 2, 3, 1)),
        jnp.transpose(coarse_tiles[:, 0], (0, 1, 3, 2)),
        speed,
        upwind,
        zone,
        jnp.transpose(rate, (1, 2, 0)),
        coarse_links,
        diffusion,
    )
    return jnp.transpose(result.reshape(4, 2, PY, 256), (1, 2, 0, 3))


def solution(mesh):
    return jax.shard_map(
        per_device,
        mesh=mesh,
        in_specs=(
            P("species", None, ("cluster", "owner"), None),
            P(),
            P(),
            P(),
            P(None, ("cluster", "owner"), None),
            P(None, "owner", None, None),
            P(),
            P(None, "cluster", None, None, "owner"),
            P(None, "cluster", None),
            P(None, "owner", None, None),
            P("species"),
            P(None, None, ("cluster", "owner"), None),
            P(None, None, ("cluster", "owner"), None),
            P(None, ("cluster", "owner"), None),
            P(),
        ),
        out_specs=P("species", None, ("cluster", "owner"), None),
        check_vma=False,
    )
```

```python
import jax
import jax.numpy as jnp
from jax import lax
from jax.experimental import pallas as pl
from jax.experimental.pallas import tpu as pltpu
from jax.sharding import PartitionSpec as P

F32 = jnp.float32
BF16 = jnp.bfloat16
I32 = jnp.int32
SWEEPS = 2
STEP = 0.1
RANK = 48
PY = 64
HIGHEST = lax.Precision.HIGHEST
NT = (((1,), (1,)), ((), ()))
TN = (((0,), (0,)), ((), ()))
NN = (((1,), (0,)), ((), ()))
FAR = [(dy, dx) for dy in range(-3, 4) for dx in range(-3, 4) if max(abs(dy), abs(dx)) >= 2]
GROUP_OFFSETS = (2, 3, -2, -3)
REACH = [(d, o) for d in (-3, 3, -2, 2, -1, 1) for o in (0, 1)] + [(0, 1)]


def dot(a, b, dims, precision=None):
    return lax.dot_general(a, b, dims, precision=precision, preferred_element_type=F32)


def lanes(shape):
    return lax.broadcasted_iota(I32, shape, len(shape) - 1)


def rows(shape):
    return lax.broadcasted_iota(I32, shape, len(shape) - 2)


def shift_rows_in_lanes(x, dy):
    if dy == 0:
        return x
    near = pltpu.roll(x, (-dy) % 128, 1)
    wrapped = pltpu.roll(x, (64 - dy) % 128, 1)
    at = lanes(x.shape) % 64 + dy
    return jnp.where((at >= 0) & (at < 64), near, wrapped)


def split_dot(a, b, dims, exact):
    whole = b if exact == 0 else a
    high = whole.astype(BF16)
    rest = (whole - high.astype(F32)).astype(BF16)
    if exact == 0:
        return dot(a, high, dims) + dot(a, rest, dims)
    return dot(high, b, dims) + dot(rest, b, dims)


def row_products(total, a, w_ref, at):
    for r in range(RANK):
        total = total + a[r : r + 1, :] * w_ref[at, r]
    return total


def both_products(totals, left, w_ref, at):
    for r in range(RANK):
        w = w_ref[at, r]
        totals = tuple(total + a[r : r + 1, :] * w for total, a in zip(totals, left))
    return totals


def kernel(
    state, near_blocks, basis_t, leaf_tiles, links, up_leaf, down_leaf, up_coarse, tiles, speed, upwind, zone,
    rate, coarse_links, diffusion,
    out,
    s0, cur, tgt, near_acc, low, oth, ctf, ctb, q, spd, upw, zon, nb, bt, lt, ltt, lk, msk, rhs,
    u_raw, d_raw, upc, upg, tcx, t2, tab, cfb, expd, fld, p1, r2,
    load_sem, load8_sem, p1_send, p1_recv, r2_send, r2_recv, halo_send, halo_recv, one_send, one_recv,
):
    cluster = lax.axis_index("cluster")
    owner = lax.axis_index("owner")
    species = lax.axis_index("species")
    n_clusters = lax.axis_size("cluster")
    group = cluster // 4
    y0 = cluster % 4
    n_groups = n_clusters // 4
    line = cluster * 2 + owner
    n_line = n_clusters * 2
    right = lax.rem(line + 1, n_line)
    left = lax.rem(line + n_line - 1, n_line)
    right_id = {"cluster": right // 2, "owner": right % 2}
    left_id = {"cluster": left // 2, "owner": left % 2}
    other_id = {"species": 1 - species}

    def ring_id(k):
        return {"cluster": group * 4 + lax.rem(y0 + k, 4)}

    def reach_id(d, o):
        return {"cluster": lax.rem(group + d + n_groups, n_groups) * 4 + y0, "owner": lax.rem(owner + o, 2)}

    r2[:, :, 7:] = jnp.zeros((SWEEPS, 2, 9, 8, 128), F32)
    barrier = pltpu.get_barrier_semaphore()
    partners = [ring_id(k) for k in (1, 2, 3)] + [reach_id(d, o) for d, o in REACH] + [left_id, right_id, other_id]
    for partner in partners:
        pl.semaphore_signal(barrier, inc=1, device_id=partner, device_id_type=pl.DeviceIdType.MESH)

    def load(src, dst, i):
        copy = pltpu.make_async_copy(src, dst, load_sem.at[i])
        copy.start()
        return copy

    state_loads = []
    for s in range(2):
        for px in range(4):
            copy = pltpu.make_async_copy(state.at[s, :, px], s0.at[px, pl.ds(64 * s, 64)], load8_sem.at[0, s * 4 + px])
            copy.start()
            state_loads.append(copy)
    bt_load = load(basis_t, bt, 0)
    u_loads = [load(up_leaf.at[px], u_raw.at[px], 1 + px) for px in range(4)]
    flow_loads = []
    for j, (src, dst) in enumerate(((speed, spd), (upwind, upw))):
        for e in range(2):
            for px in range(4):
                copy = pltpu.make_async_copy(src.at[e, :, px], dst.at[e, px], load8_sem.at[1 + j, e * 4 + px])
                copy.start()
                flow_loads.append(copy)
    tiles_load = load(tiles, tcx.at[:, :, owner], 5)
    lk_load = load(links, lk, 7)
    upc_load = load(up_coarse, upc, 8)
    lt_load = load(leaf_tiles, lt, 9)
    zone_loads = []
    for px in range(4):
        copy = pltpu.make_async_copy(zone.at[:, px], zon.at[px], load8_sem.at[3, px])
        copy.start()
        zone_loads.append(copy)
    nb_load = load(near_blocks, nb, 6)
    d_loads = [load(down_leaf.at[px], d_raw.at[px], 10 + px) for px in range(4)]

    def remote(src, dst, send, recv, device_id):
        return pltpu.make_async_remote_copy(
            src_ref=src, dst_ref=dst, send_sem=send, recv_sem=recv,
            device_id=device_id, device_id_type=pl.DeviceIdType.MESH,
        )

    scale_0 = STEP * diffusion[0]
    scale_1 = STEP * diffusion[1]
    scale = jnp.where(lax.broadcasted_iota(I32, (128, 1), 0) < 64, scale_0, scale_1)

    tab[...] = jnp.zeros_like(tab)

    def own_columns(k, src):
        for px in range(4):
            v = src[px].astype(BF16)
            low[k, px + 1] = v
            coeffs = dot(bt[...], v, NT)
            ctf[0, px] = coeffs[:, :64]
            ctf[1, px] = coeffs[:, 64:]
            ctb[k, px + 3] = coeffs.astype(BF16)

    def halo_copies(k):
        h, g = halo_send, halo_recv
        return [
            remote(low.at[k, 4], low.at[k, 0], h.at[k, 0], g.at[k, 0], right_id),
            remote(low.at[k, 1], low.at[k, 5], h.at[k, 1], g.at[k, 1], left_id),
            remote(ctb.at[k, pl.ds(4, 3)], ctb.at[k, pl.ds(0, 3)], h.at[k, 2], g.at[k, 2], right_id),
            remote(ctb.at[k, pl.ds(3, 3)], ctb.at[k, pl.ds(7, 3)], h.at[k, 3], g.at[k, 3], left_id),
        ]

    def root_tile(total):
        pick_row = rows((8, 128)) - 2 * y0
        pick = jnp.where((pick_row >= 0) & (pick_row < 2) & (lanes((8, 128)) // 64 == pick_row), 1.0, 0.0).astype(BF16)
        padded = jnp.concatenate([total, jnp.zeros((128 - RANK, 128), F32)], axis=0)
        return split_dot(pick, padded, NT, 0)

    def send_roots(k):
        copies = [remote(p1.at[k, 0], p1.at[k, j], p1_send.at[k, j], p1_recv.at[k, j], ring_id(j)) for j in (2, 1, 3)]
        for copy in copies:
            copy.start()
        return copies

    def send_groups(k, copies):
        for copy in copies:
            copy.wait_recv()
        tile = p1[k, 0]
        for j in (1, 2, 3):
            tile = tile + p1[k, j]
        r2[k, 0, 3] = tile
        sends = [
            remote(r2.at[k, 0, 3], r2.at[k, o, 3 - d], r2_send.at[k, i], r2_recv.at[k, i], reach_id(d, o))
            for i, (d, o) in enumerate(REACH)
        ]
        for copy in sends:
            copy.start()
        return sends

    def near(k, columns):
        for dy in (0, -1, 1):
            wide = jnp.concatenate(
                [jnp.concatenate([low[k, px + dx + 1] for px in columns], axis=0) for dx in (-1, 0, 1)], axis=1
            )
            at = 3 * (dy + 1)
            part = dot(wide, nb[at : at + 3].reshape(768, 256), NN)
            for b, px in enumerate(columns):
                for s in range(2):
                    block = part[128 * b + 64 * s : 128 * b + 64 * s + 64]
                    if dy == 0:
                        near_acc[px, pl.ds(64 * s, 64)] = block
                    else:
                        near_acc[px, pl.ds(64 * s, 64)] += pltpu.roll(block, (-dy) % 64, 0)

    def leaf(k):
        first = 0
        for dy in range(-3, 4):
            mine = [dx for y, dx in FAR if y == dy]
            n = len(mine)
            side = (dy + 3) % 2
            for px in range(4):
                for i, dx in enumerate(mine):
                    coeffs = ctb[k, px + 3 + dx].reshape(3, 16, 128)
                    masked = coeffs * msk[px, first + i][None]
                    rhs[side, pl.ds(i * RANK, RANK), pl.ds(px * 128, 128)] = masked.reshape(RANK, 128)
            part = dot(ltt[:, first * RANK : (first + n) * RANK], rhs[side, : n * RANK, :], NN)
            for px in range(4):
                piece = shift_rows_in_lanes(part[:, px * 128 : px * 128 + 128], dy)
                if first == 0:
                    expd[px] = piece
                else:
                    expd[px] += piece
            first += n

    def prepare_masks():
        def column(px, _):
            both = jnp.concatenate([lk[px].astype(F32)] * 2, axis=1)
            first = 0
            for dy in range(-3, 4):
                n = sum(1 for y, _ in FAR if y == dy)
                turned = shift_rows_in_lanes(both[first : first + n], -dy)
                for i in range(n):
                    msk[px, first + i] = jnp.broadcast_to(turned[i : i + 1], (16, 128)).astype(BF16)
                first += n
            return 0

        lax.fori_loop(0, 4, column, 0)

    def prepare_leaf_tiles():
        first = 0
        for dy in range(-3, 4):
            n = sum(1 for y, _ in FAR if y == dy)
            stacked = lt[first : first + n].reshape(n * RANK, RANK)
            ltt[:, first * RANK : (first + n) * RANK] = jnp.swapaxes(stacked, 0, 1).astype(BF16)
            first += n

    def prepare_coarse():
        lane = lanes((64, 128))
        at_group = group + lane // 8 - 3 + n_groups
        at_y = (lane // 2) % 4
        for i, target in enumerate(((4 * at_group + at_y) % n_clusters, (2 * at_group + at_y // 2) % (n_clusters // 2))):
            pick = jnp.where((rows((64, 128)) == target) & (lane < 56), 1.0, 0.0).astype(BF16)

            def block(b, _, pick=pick, i=i):
                x = upc[i, pl.ds(b * 8, 8)].reshape(8 * RANK, 64).astype(BF16)
                upg[i, pl.ds(b * 8, 8)] = dot(x, pick, NN).reshape(8, RANK, 128)
                return 0

            lax.fori_loop(0, RANK // 8, block, 0)
    def prepare_coarse_tiles():
        t2[...] = jnp.zeros_like(t2)
        for l in range(3):
            for k in range(4):
                at = (l * 4 + k) * 64
                whole = tcx[l, k].reshape(RANK, RANK)
                high = whole.astype(BF16)
                t2[0, :, at : at + RANK] = high
                t2[1, :, at : at + RANK] = (whole - high.astype(F32)).astype(BF16)

    def coarse(k):
        zero = jnp.zeros((RANK, 128), F32)
        lane = lanes((1, 128))
        at_d, at_y = lane // 8 - 3, (lane // 2) % 4
        wide_lane = lanes((RANK, 128))
        values = jnp.swapaxes((r2[k, 0] + r2[k, 1]).reshape(128, 128), 0, 1)[:RANK]
        pieces = []
        for l in range(3):
            if l > 0:
                raised = row_products(zero, values, upg, l - 1)
                hop = 2 * l
                sibling = jnp.where((wide_lane // hop) % 2 == 0, pltpu.roll(raised, 128 - hop, 1), pltpu.roll(raised, hop, 1))
                values = raised + sibling
            for i, offset in enumerate(GROUP_OFFSETS):
                if l == 0:
                    hit = at_d * 4 + at_y == y0 + offset
                elif l == 1:
                    hit = (at_d * 2 + at_y // 2 == y0 // 2 + offset) & (at_y % 2 == 0)
                else:
                    hit = (at_d == offset) & (at_y == 0)
                hit = hit & (lane < 56)
                pieces.append(values * jnp.where(hit, coarse_links[l, 0, i].astype(F32), 0.0))
                pieces.append(jnp.zeros((16, 128), F32))
        stacked = jnp.concatenate(pieces, axis=0)
        high = stacked.astype(BF16)
        rest = (stacked - high.astype(F32)).astype(BF16)
        found = dot(t2[0], high, NN) + (dot(t2[0], rest, NN) + dot(t2[1], high, NN))
        spread = jnp.where(rows((128, 256)) % 2 == lanes((128, 256)) // 128, 1.0, 0.0).astype(BF16)
        both = split_dot(found, spread, NN, 1)
        cfb[0] = both[:, :64]
        cfb[1] = both[:, 128:192]

    def finish(src, dst, inverse_diag):
        def expand(px, _):
            zero = jnp.zeros((RANK, 64), F32)
            expanded = both_products((zero, zero), (cfb[0], cfb[1]), d_raw, px)
            fld[px] = (expd[px] + jnp.concatenate(expanded, axis=1)).astype(BF16)
            return 0

        lax.fori_loop(0, 4, expand, 0)
        for px in range(4):
            applied = near_acc[px] + dot(fld[px], bt[...], TN)
            v = src[px]
            dst[px] = v + (tgt[px] - v - scale * applied) * inverse_diag

    def reaction(px, _):
        z = zon[px]
        values = [jnp.tanh(s0[px, :64]), jnp.tanh(s0[px, 64:])]
        there = oth[px].astype(F32)
        values += [jnp.tanh(there[:64]), jnp.tanh(there[64:])]
        for s in range(2):
            total = jnp.zeros((64, 256), F32)
            for t in range(4):
                table = jnp.broadcast_to(tab[4 * s + t : 4 * s + t + 1, :], (64, 128))
                found = [jnp.take_along_axis(table, z[:, h : h + 128], axis=1) for h in (0, 128)]
                total = total + jnp.concatenate(found, axis=1) * values[t]
            tgt[px, pl.ds(64 * s, 64)] = s0[px, pl.ds(64 * s, 64)] + STEP * total
        return 0

    def advection(s, _):
        at = pl.ds(pl.multiple_of(s * 64, 64), 64)
        n = lanes((64, 256))

        def flux_x(px):
            v = low[0, px + 1, at].astype(F32)
            before = low[0, px, at].astype(F32)
            v_left = pltpu.roll(jnp.where(n % 16 == 15, pltpu.roll(before, 256 - 16, 1), v), 1, 1)
            w = q[0, px]
            return v, w * jnp.where(w > 0, v_left, v)

        v, flux = flux_x(0)
        for px in range(4):
            v_next, flux_next = flux_x(px + 1)
            flux_right = pltpu.roll(jnp.where(n % 16 == 0, pltpu.roll(flux_next, 16, 1), flux), 255, 1)
            v_up = pltpu.roll(jnp.where(n >= 240, pltpu.roll(v, 1, 0), v), 16, 1)
            w = q[1, px]
            flux_y = w * jnp.where(w > 0, v_up, v)
            flux_down = pltpu.roll(jnp.where(n < 16, pltpu.roll(flux_y, 63, 0), flux_y), 256 - 16, 1)
            tgt[px, at] += STEP * (flux - flux_right + flux_y - flux_down)
            v, flux = v_next, flux_next
        return 0

    for copy in state_loads:
        copy.wait()
    bt_load.wait()
    own_columns(0, s0)
    for copy in u_loads:
        copy.wait()

    def roots():
        totals = lax.fori_loop(
            0, 4, lambda px, t: both_products(t, (ctf[0, px], ctf[1, px]), u_raw, px), (jnp.zeros((RANK, 64), F32),) * 2
        )
        return jnp.concatenate(totals, axis=1)

    p1[0, 0] = root_tile(roots())
    pl.semaphore_wait(barrier, len(partners))
    ring = send_roots(0)
    halos = halo_copies(0)
    others = remote(low.at[0, pl.ds(1, 4)], oth, one_send.at[0], one_recv.at[0], other_id)
    for copy in halos:
        copy.start()
    others.start()
    for copy in flow_loads:
        copy.wait()

    def signed(px, _):
        for e in range(2):
            v = spd[e, px]
            q[e, px] = jnp.where(upw[e, px] == 0, v, -v)
        return 0

    lax.fori_loop(0, 4, signed, 0)
    edge = remote(q.at[0, 0], q.at[0, 4], one_send.at[2], one_recv.at[2], left_id)
    edge.start()
    tiles_load.wait()
    tile_copy = remote(tcx.at[:, :, owner], tcx.at[:, :, owner], one_send.at[1], one_recv.at[1], {"owner": 1 - owner})
    tile_copy.start()

    lk_load.wait()
    prepare_masks()
    lt_load.wait()
    prepare_leaf_tiles()
    upc_load.wait()
    prepare_coarse()
    reach = send_groups(0, ring)

    for s in range(2):
        for t in range(4):
            at = (2 * species + t) % 4
            tab[4 * s + t : 4 * s + t + 1, :16] = rate[2 * species + s, pl.ds(at, 1), :]
    for copy in zone_loads:
        copy.wait()
    others.wait_recv()
    lax.fori_loop(0, 4, reaction, 0)
    for copy in halos:
        copy.wait_recv()
    edge.wait_recv()
    lax.fori_loop(0, 2, advection, 0)
    nb_load.wait()
    near(0, (0, 1, 2, 3))
    eye = rows((256, 256)) == lanes((256, 256))
    diag = jnp.sum(jnp.where(eye, nb[4].astype(F32), 0.0), axis=0, keepdims=True)
    inverse_diag = 1.0 / (1.0 + scale * diag)
    leaf(0)
    tile_copy.wait_recv()
    prepare_coarse_tiles()
    for copy in d_loads:
        copy.wait()
    for copy in reach:
        copy.wait_recv()
    coarse(0)
    finish(s0, cur, inverse_diag)

    own_columns(1, cur)
    halos_1 = halo_copies(1)
    p1[1, 0] = root_tile(roots())
    ring_1 = send_roots(1)
    for copy in halos_1:
        copy.start()
    near(1, (1, 2))
    reach_1 = send_groups(1, ring_1)
    for copy in halos_1:
        copy.wait_recv()
    near(1, (0, 3))
    leaf(1)
    for copy in reach_1:
        copy.wait_recv()
    coarse(1)
    finish(cur, out, inverse_diag)

    for copy in halos + halos_1 + [others, tile_copy, edge] + ring + ring_1 + reach + reach_1:
        copy.wait_send()


def per_device(
    state, near_blocks, basis, leaf_tiles, leaf_links, up_leaf, up_coarse, coarse_tiles, coarse_links,
    down_leaf, diffusion, speed, upwind, zone, rate,
):
    anywhere = pl.BlockSpec(memory_space=pl.ANY)
    vmem = pl.BlockSpec(memory_space=pltpu.VMEM)
    smem = pl.BlockSpec(memory_space=pltpu.SMEM)
    dma = pltpu.SemaphoreType.DMA
    scratch = [
        pltpu.VMEM((4, 128, 256), F32),
        pltpu.VMEM((4, 128, 256), F32),
        pltpu.VMEM((4, 128, 256), F32),
        pltpu.VMEM((4, 128, 256), F32),
        pltpu.VMEM((2, 6, 128, 256), BF16),
        pltpu.VMEM((4, 128, 256), BF16),
        pltpu.VMEM((2, 4, RANK, 64), F32),
        pltpu.VMEM((2, 10, RANK, 128), BF16),
        pltpu.VMEM((2, 5, 64, 256), F32),
        pltpu.VMEM((2, 4, 64, 256), F32),
        pltpu.VMEM((2, 4, 64, 256), I32),
        pltpu.VMEM((4, 64, 256), I32),
        pltpu.VMEM((9, 256, 256), BF16),
        pltpu.VMEM((RANK, 256), BF16),
        pltpu.VMEM((40, RANK, RANK), F32),
        pltpu.VMEM((RANK, 40 * RANK), BF16),
        pltpu.VMEM((4, 40, 64), I32),
        pltpu.VMEM((4, 40, 16, 128), BF16),
        pltpu.VMEM((2, 7 * RANK, 512), BF16),
        pltpu.VMEM((4, RANK, RANK, 64), F32),
        pltpu.VMEM((4, RANK, RANK, 64), F32),
        pltpu.VMEM((2, RANK, RANK, 64), F32),
        pltpu.VMEM((2, RANK, RANK, 128), F32),
        pltpu.VMEM((3, 4, 2, 24, RANK), F32),
        pltpu.VMEM((2, RANK, 12 * 64), BF16),
        pltpu.VMEM((8, 128), F32),
        pltpu.VMEM((2, RANK, 64), F32),
        pltpu.VMEM((4, RANK, 128), F32),
        pltpu.VMEM((4, RANK, 128), BF16),
        pltpu.VMEM((2, 4, 8, 128), F32),
        pltpu.VMEM((2, 2, 16, 8, 128), F32),
        dma((14,)),
        dma((4, 8)),
        dma((2, 4)),
        dma((2, 4)),
        dma((2, 13)),
        dma((2, 13)),
        dma((2, 4)),
        dma((2, 4)),
        dma((3,)),
        dma((3,)),
    ]
    result = pl.pallas_call(
        kernel,
        out_shape=pltpu.VMEM((4, 128, 256), F32),
        in_specs=[anywhere] * 12 + [vmem, smem, smem],
        out_specs=vmem,
        scratch_shapes=scratch,
        compiler_params=pltpu.CompilerParams(
            collective_id=0, has_side_effects=True, vmem_limit_bytes=56 * 1024 * 1024
        ),
    )(
        state,
        near_blocks,
        basis.T,
        leaf_tiles,
        jnp.transpose(leaf_links, (1, 2, 0)),
        jnp.transpose(up_leaf, (1, 2, 3, 0)),
        jnp.transpose(down_leaf, (1, 2, 3, 0)),
        jnp.transpose(up_coarse, (0, 2, 3, 1)),
        jnp.transpose(coarse_tiles[:, 0], (0, 1, 3, 2)),
        speed,
        upwind,
        zone,
        jnp.transpose(rate, (1, 2, 0)),
        coarse_links,
        diffusion,
    )
    return jnp.transpose(result.reshape(4, 2, PY, 256), (1, 2, 0, 3))


def solution(mesh):
    return jax.shard_map(
        per_device,
        mesh=mesh,
        in_specs=(
            P("species", None, ("cluster", "owner"), None),
            P(),
            P(),
            P(),
            P(None, ("cluster", "owner"), None),
            P(None, "owner", None, None),
            P(),
            P(None, "cluster", None, None, "owner"),
            P(None, "cluster", None),
            P(None, "owner", None, None),
            P("species"),
            P(None, None, ("cluster", "owner"), None),
            P(None, None, ("cluster", "owner"), None),
            P(None, ("cluster", "owner"), None),
            P(),
        ),
        out_specs=P("species", None, ("cluster", "owner"), None),
        check_vma=False,
    )
```

```python
import jax
import jax.numpy as jnp
from jax import lax
from jax.experimental import pallas as pl
from jax.experimental.pallas import tpu as pltpu
from jax.sharding import PartitionSpec as P

F32 = jnp.float32
BF16 = jnp.bfloat16
I32 = jnp.int32
SWEEPS = 2
STEP = 0.1
RANK = 48
PY = 64
HIGHEST = lax.Precision.HIGHEST
NT = (((1,), (1,)), ((), ()))
TN = (((0,), (0,)), ((), ()))
NN = (((1,), (0,)), ((), ()))
FAR = [(dy, dx) for dy in range(-3, 4) for dx in range(-3, 4) if max(abs(dy), abs(dx)) >= 2]
GROUP_OFFSETS = (2, 3, -2, -3)
REACH = [(d, o) for d in (-3, 3, -2, 2, -1, 1) for o in (0, 1)] + [(0, 1)]


def dot(a, b, dims, precision=None):
    return lax.dot_general(a, b, dims, precision=precision, preferred_element_type=F32)


def lanes(shape):
    return lax.broadcasted_iota(I32, shape, len(shape) - 1)


def rows(shape):
    return lax.broadcasted_iota(I32, shape, len(shape) - 2)


def shift_rows_in_lanes(x, dy):
    if dy == 0:
        return x
    near = pltpu.roll(x, (-dy) % 128, 1)
    wrapped = pltpu.roll(x, (64 - dy) % 128, 1)
    at = lanes(x.shape) % 64 + dy
    return jnp.where((at >= 0) & (at < 64), near, wrapped)


def split_dot(a, b, dims, exact):
    whole = b if exact == 0 else a
    high = whole.astype(BF16)
    rest = (whole - high.astype(F32)).astype(BF16)
    if exact == 0:
        return dot(a, high, dims) + dot(a, rest, dims)
    return dot(high, b, dims) + dot(rest, b, dims)


def row_products(total, a, w_ref, at):
    for r in range(RANK):
        total = total + a[r : r + 1, :] * w_ref[at, r]
    return total


def both_products(totals, left, w_ref, at):
    for r in range(RANK):
        w = w_ref[at, r]
        totals = tuple(total + a[r : r + 1, :] * w for total, a in zip(totals, left))
    return totals


def kernel(
    state, near_blocks, basis_t, leaf_tiles, links, up_leaf, down_leaf, up_coarse, tiles, speed, upwind, zone,
    rate, coarse_links, diffusion,
    out,
    s0, cur, tgt, near_acc, low, oth, ctf, ctb, q, spd, upw, zon, nb, bt, lt, ltt, lk, msk, rhs,
    u_raw, u_wide, d_raw, d_wide, ctw, upc, upg, tcx, t2, tab, cfb, expd, fld, p1, r2,
    load_sem, load8_sem, p1_send, p1_recv, r2_send, r2_recv, halo_send, halo_recv, one_send, one_recv,
):
    cluster = lax.axis_index("cluster")
    owner = lax.axis_index("owner")
    species = lax.axis_index("species")
    n_clusters = lax.axis_size("cluster")
    group = cluster // 4
    y0 = cluster % 4
    n_groups = n_clusters // 4
    line = cluster * 2 + owner
    n_line = n_clusters * 2
    right = lax.rem(line + 1, n_line)
    left = lax.rem(line + n_line - 1, n_line)
    right_id = {"cluster": right // 2, "owner": right % 2}
    left_id = {"cluster": left // 2, "owner": left % 2}
    other_id = {"species": 1 - species}

    def ring_id(k):
        return {"cluster": group * 4 + lax.rem(y0 + k, 4)}

    def reach_id(d, o):
        return {"cluster": lax.rem(group + d + n_groups, n_groups) * 4 + y0, "owner": lax.rem(owner + o, 2)}

    r2[:, :, 7:] = jnp.zeros((SWEEPS, 2, 9, 8, 128), F32)
    barrier = pltpu.get_barrier_semaphore()
    partners = [ring_id(k) for k in (1, 2, 3)] + [reach_id(d, o) for d, o in REACH] + [left_id, right_id, other_id]
    for partner in partners:
        pl.semaphore_signal(barrier, inc=1, device_id=partner, device_id_type=pl.DeviceIdType.MESH)

    def load(src, dst, i):
        copy = pltpu.make_async_copy(src, dst, load_sem.at[i])
        copy.start()
        return copy

    state_loads = []
    for s in range(2):
        for px in range(4):
            copy = pltpu.make_async_copy(state.at[s, :, px], s0.at[px, pl.ds(64 * s, 64)], load8_sem.at[0, s * 4 + px])
            copy.start()
            state_loads.append(copy)
    bt_load = load(basis_t, bt, 0)
    u_loads = [load(up_leaf.at[px], u_raw.at[px], 1 + px) for px in range(4)]
    flow_loads = []
    for j, (src, dst) in enumerate(((speed, spd), (upwind, upw))):
        for e in range(2):
            for px in range(4):
                copy = pltpu.make_async_copy(src.at[e, :, px], dst.at[e, px], load8_sem.at[1 + j, e * 4 + px])
                copy.start()
                flow_loads.append(copy)
    def remote(src, dst, send, recv, device_id):
        return pltpu.make_async_remote_copy(
            src_ref=src, dst_ref=dst, send_sem=send, recv_sem=recv,
            device_id=device_id, device_id_type=pl.DeviceIdType.MESH,
        )

    scale_0 = STEP * diffusion[0]
    scale_1 = STEP * diffusion[1]
    scale = jnp.where(lax.broadcasted_iota(I32, (128, 1), 0) < 64, scale_0, scale_1)

    tab[...] = jnp.zeros_like(tab)

    def own_columns(k, src):
        for px in range(4):
            v = src[px].astype(BF16)
            low[k, px + 1] = v
            coeffs = dot(bt[...], v, NT)
            if k == 0:
                ctf[0, px] = coeffs[:, :64]
                ctf[1, px] = coeffs[:, 64:]
            elif px % 2 == 0:
                even = coeffs
            else:
                ctw[0, px // 2] = jnp.concatenate([even[:, :64], coeffs[:, :64]], axis=1)
                ctw[1, px // 2] = jnp.concatenate([even[:, 64:], coeffs[:, 64:]], axis=1)
            ctb[k, px + 3] = coeffs.astype(BF16)

    def halo_copies(k):
        h, g = halo_send, halo_recv
        return [
            remote(low.at[k, 4], low.at[k, 0], h.at[k, 0], g.at[k, 0], right_id),
            remote(low.at[k, 1], low.at[k, 5], h.at[k, 1], g.at[k, 1], left_id),
            remote(ctb.at[k, pl.ds(4, 3)], ctb.at[k, pl.ds(0, 3)], h.at[k, 2], g.at[k, 2], right_id),
            remote(ctb.at[k, pl.ds(3, 3)], ctb.at[k, pl.ds(7, 3)], h.at[k, 3], g.at[k, 3], left_id),
        ]

    def root_tile(totals):
        total = jnp.concatenate(totals, axis=1)
        width = total.shape[1]
        pick_row = rows((8, width)) - 2 * y0
        mine = (pick_row >= 0) & (pick_row < 2) & (lanes((8, width)) // (width // 2) == pick_row)
        padded = jnp.concatenate([total, jnp.zeros((128 - RANK, width), F32)], axis=0)
        return split_dot(jnp.where(mine, 1.0, 0.0).astype(BF16), padded, NT, 0)

    def send_roots(k):
        copies = [remote(p1.at[k, 0], p1.at[k, j], p1_send.at[k, j], p1_recv.at[k, j], ring_id(j)) for j in (2, 1, 3)]
        for copy in copies:
            copy.start()
        return copies

    def send_groups(k, copies):
        for copy in copies:
            copy.wait_recv()
        tile = p1[k, 0]
        for j in (1, 2, 3):
            tile = tile + p1[k, j]
        r2[k, 0, 3] = tile
        sends = [
            remote(r2.at[k, 0, 3], r2.at[k, o, 3 - d], r2_send.at[k, i], r2_recv.at[k, i], reach_id(d, o))
            for i, (d, o) in enumerate(REACH)
        ]
        for copy in sends:
            copy.start()
        return sends

    def near(k, columns):
        for dy in (0, -1, 1):
            wide = jnp.concatenate(
                [jnp.concatenate([low[k, px + dx + 1] for px in columns], axis=0) for dx in (-1, 0, 1)], axis=1
            )
            at = 3 * (dy + 1)
            part = dot(wide, nb[at : at + 3].reshape(768, 256), NN)
            for b, px in enumerate(columns):
                for s in range(2):
                    block = part[128 * b + 64 * s : 128 * b + 64 * s + 64]
                    if dy == 0:
                        near_acc[px, pl.ds(64 * s, 64)] = block
                    else:
                        near_acc[px, pl.ds(64 * s, 64)] += pltpu.roll(block, (-dy) % 64, 0)

    def leaf(k):
        first = 0
        for dy in range(-3, 4):
            mine = [dx for y, dx in FAR if y == dy]
            n = len(mine)
            side = (dy + 3) % 2
            for px in range(4):
                for i, dx in enumerate(mine):
                    coeffs = ctb[k, px + 3 + dx].reshape(3, 16, 128)
                    masked = coeffs * msk[px, first + i][None]
                    rhs[side, pl.ds(i * RANK, RANK), pl.ds(px * 128, 128)] = masked.reshape(RANK, 128)
            part = dot(ltt[:, first * RANK : (first + n) * RANK], rhs[side, : n * RANK, :], NN)
            for px in range(4):
                piece = shift_rows_in_lanes(part[:, px * 128 : px * 128 + 128], dy)
                if first == 0:
                    expd[px] = piece
                else:
                    expd[px] += piece
            first += n

    def prepare_masks():
        def column(px, _):
            both = jnp.concatenate([lk[px].astype(F32)] * 2, axis=1)
            first = 0
            for dy in range(-3, 4):
                n = sum(1 for y, _ in FAR if y == dy)
                turned = shift_rows_in_lanes(both[first : first + n], -dy)
                for i in range(n):
                    msk[px, first + i] = jnp.broadcast_to(turned[i : i + 1], (16, 128)).astype(BF16)
                first += n
            return 0

        lax.fori_loop(0, 4, column, 0)

    def prepare_leaf_tiles():
        first = 0
        for dy in range(-3, 4):
            n = sum(1 for y, _ in FAR if y == dy)
            stacked = lt[first : first + n].reshape(n * RANK, RANK)
            ltt[:, first * RANK : (first + n) * RANK] = jnp.swapaxes(stacked, 0, 1).astype(BF16)
            first += n

    def prepare_coarse():
        lane = lanes((64, 128))
        at_group = group + lane // 8 - 3 + n_groups
        at_y = (lane // 2) % 4
        for i, target in enumerate(((4 * at_group + at_y) % n_clusters, (2 * at_group + at_y // 2) % (n_clusters // 2))):
            pick = jnp.where((rows((64, 128)) == target) & (lane < 56), 1.0, 0.0).astype(BF16)

            for r in range(0, RANK, 8):
                x = upc[i, r : r + 8].reshape(8 * RANK, 64).astype(BF16)
                upg[i, r : r + 8] = dot(x, pick, NN).reshape(8, RANK, 128)
    def prepare_coarse_tiles():
        t2[...] = jnp.zeros_like(t2)
        for l in range(3):
            for k in range(4):
                at = (l * 4 + k) * 64
                whole = tcx[l, k].reshape(RANK, RANK)
                high = whole.astype(BF16)
                t2[0, :, at : at + RANK] = high
                t2[1, :, at : at + RANK] = (whole - high.astype(F32)).astype(BF16)

    def coarse(k):
        zero = jnp.zeros((RANK, 128), F32)
        lane = lanes((1, 128))
        at_d, at_y = lane // 8 - 3, (lane // 2) % 4
        wide_lane = lanes((RANK, 128))
        values = jnp.swapaxes((r2[k, 0] + r2[k, 1]).reshape(128, 128), 0, 1)[:RANK]
        pieces = []
        for l in range(3):
            if l > 0:
                raised = row_products(zero, values, upg, l - 1)
                hop = 2 * l
                sibling = jnp.where((wide_lane // hop) % 2 == 0, pltpu.roll(raised, 128 - hop, 1), pltpu.roll(raised, hop, 1))
                values = raised + sibling
            for i, offset in enumerate(GROUP_OFFSETS):
                if l == 0:
                    hit = at_d * 4 + at_y == y0 + offset
                elif l == 1:
                    hit = (at_d * 2 + at_y // 2 == y0 // 2 + offset) & (at_y % 2 == 0)
                else:
                    hit = (at_d == offset) & (at_y == 0)
                hit = hit & (lane < 56)
                pieces.append(values * jnp.where(hit, coarse_links[l, 0, i].astype(F32), 0.0))
                pieces.append(jnp.zeros((16, 128), F32))
        stacked = jnp.concatenate(pieces, axis=0)
        high = stacked.astype(BF16)
        rest = (stacked - high.astype(F32)).astype(BF16)
        found = dot(t2[0], high, NN) + (dot(t2[0], rest, NN) + dot(t2[1], high, NN))
        spread = jnp.where(rows((128, 256)) % 2 == lanes((128, 256)) // 128, 1.0, 0.0).astype(BF16)
        both = split_dot(found, spread, NN, 1)
        cfb[0] = both[:, :128]
        cfb[1] = both[:, 128:]

    def expand(j, _):
        zero = jnp.zeros((RANK, 128), F32)
        e0, e1 = both_products((zero, zero), (cfb[0], cfb[1]), d_wide, j)
        for i in range(2):
            half = slice(64 * i, 64 * i + 64)
            expanded = jnp.concatenate([e0[:, half], e1[:, half]], axis=1)
            fld[2 * j + i] = (expd[2 * j + i] + expanded).astype(BF16)
        return 0

    def prepare_finish(src, inverse_diag):
        def column(px, _):
            v = src[px]
            near_acc[px] = v + (tgt[px] - v - scale * near_acc[px]) * inverse_diag
            return 0

        lax.fori_loop(0, 4, column, 0)

    def finish(dst, weight):
        lax.fori_loop(0, 2, expand, 0)
        for px in range(4):
            dst[px] = near_acc[px] - weight * dot(fld[px], bt[...], TN)

    def reaction(px, _):
        z = zon[px]
        values = [jnp.tanh(s0[px, :64]), jnp.tanh(s0[px, 64:])]
        there = oth[px].astype(F32)
        values += [jnp.tanh(there[:64]), jnp.tanh(there[64:])]
        for s in range(2):
            total = jnp.zeros((64, 256), F32)
            for t in range(4):
                table = jnp.broadcast_to(tab[4 * s + t : 4 * s + t + 1, :], (64, 128))
                found = [jnp.take_along_axis(table, z[:, h : h + 128], axis=1) for h in (0, 128)]
                total = total + jnp.concatenate(found, axis=1) * values[t]
            tgt[px, pl.ds(64 * s, 64)] = s0[px, pl.ds(64 * s, 64)] + STEP * total
        return 0

    def advection(s, _):
        at = pl.ds(pl.multiple_of(s * 64, 64), 64)
        n = lanes((64, 256))

        def flux_x(px):
            v = low[0, px + 1, at].astype(F32)
            before = low[0, px, at].astype(F32)
            v_left = pltpu.roll(jnp.where(n % 16 == 15, pltpu.roll(before, 256 - 16, 1), v), 1, 1)
            w = q[0, px]
            return v, w * jnp.where(w > 0, v_left, v)

        v, flux = flux_x(0)
        for px in range(4):
            v_next, flux_next = flux_x(px + 1)
            flux_right = pltpu.roll(jnp.where(n % 16 == 0, pltpu.roll(flux_next, 16, 1), flux), 255, 1)
            v_up = pltpu.roll(jnp.where(n >= 240, pltpu.roll(v, 1, 0), v), 16, 1)
            w = q[1, px]
            flux_y = w * jnp.where(w > 0, v_up, v)
            flux_down = pltpu.roll(jnp.where(n < 16, pltpu.roll(flux_y, 63, 0), flux_y), 256 - 16, 1)
            tgt[px, at] += STEP * (flux - flux_right + flux_y - flux_down)
            v, flux = v_next, flux_next
        return 0

    for copy in state_loads:
        copy.wait()
    bt_load.wait()
    own_columns(0, s0)
    for copy in u_loads:
        copy.wait()
    tiles_load = load(tiles, tcx.at[:, :, owner], 5)
    lk_load = load(links, lk, 7)
    upc_load = load(up_coarse, upc, 8)
    lt_load = load(leaf_tiles, lt, 9)
    zone_loads = []
    for px in range(4):
        copy = pltpu.make_async_copy(zone.at[:, px], zon.at[px], load8_sem.at[3, px])
        copy.start()
        zone_loads.append(copy)
    nb_load = load(near_blocks, nb, 6)
    d_loads = [load(down_leaf.at[px], d_raw.at[px], 10 + px) for px in range(4)]


    def roots():
        totals = lax.fori_loop(
            0, 4, lambda px, t: both_products(t, (ctf[0, px], ctf[1, px]), u_raw, px), (jnp.zeros((RANK, 64), F32),) * 2
        )
        return totals

    def wide_roots():
        zero = jnp.zeros((RANK, 128), F32)
        return lax.fori_loop(
            0, 2, lambda j, t: both_products(t, (ctw[0, j], ctw[1, j]), u_wide, j), (zero, zero)
        )

    def pack(raw, wide):
        def pair(j, _):
            for r in range(RANK):
                wide[j, r] = jnp.concatenate([raw[2 * j, r], raw[2 * j + 1, r]], axis=1)
            return 0

        lax.fori_loop(0, 2, pair, 0)

    p1[0, 0] = root_tile(roots())
    pl.semaphore_wait(barrier, len(partners))
    ring = send_roots(0)
    halos = halo_copies(0)
    others = remote(low.at[0, pl.ds(1, 4)], oth, one_send.at[0], one_recv.at[0], other_id)
    for copy in halos:
        copy.start()
    others.start()
    for copy in flow_loads:
        copy.wait()

    def signed(px, _):
        for e in range(2):
            v = spd[e, px]
            q[e, px] = jnp.where(upw[e, px] == 0, v, -v)
        return 0

    lax.fori_loop(0, 4, signed, 0)
    edge = remote(q.at[0, 0], q.at[0, 4], one_send.at[2], one_recv.at[2], left_id)
    edge.start()
    tiles_load.wait()
    tile_copy = remote(tcx.at[:, :, owner], tcx.at[:, :, owner], one_send.at[1], one_recv.at[1], {"owner": 1 - owner})
    tile_copy.start()

    lk_load.wait()
    prepare_masks()
    lt_load.wait()
    prepare_leaf_tiles()
    upc_load.wait()
    prepare_coarse()
    reach = send_groups(0, ring)

    for s in range(2):
        for t in range(4):
            at = (2 * species + t) % 4
            tab[4 * s + t : 4 * s + t + 1, :16] = rate[2 * species + s, pl.ds(at, 1), :]
    for copy in zone_loads:
        copy.wait()
    others.wait_recv()
    lax.fori_loop(0, 4, reaction, 0)
    for copy in halos:
        copy.wait_recv()
    edge.wait_recv()
    lax.fori_loop(0, 2, advection, 0)
    nb_load.wait()
    near(0, (0, 1, 2, 3))
    eye = rows((256, 256)) == lanes((256, 256))
    diag = jnp.sum(jnp.where(eye, nb[4].astype(F32), 0.0), axis=0, keepdims=True)
    inverse_diag = 1.0 / (1.0 + scale * diag)
    weight = scale * inverse_diag
    leaf(0)
    tile_copy.wait_recv()
    prepare_coarse_tiles()
    pack(u_raw, u_wide)
    for copy in d_loads:
        copy.wait()
    pack(d_raw, d_wide)
    prepare_finish(s0, inverse_diag)
    for copy in reach:
        copy.wait_recv()
    coarse(0)
    finish(cur, weight)

    own_columns(1, cur)
    halos_1 = halo_copies(1)
    p1[1, 0] = root_tile(wide_roots())
    ring_1 = send_roots(1)
    for copy in halos_1:
        copy.start()
    near(1, (1, 2))
    reach_1 = send_groups(1, ring_1)
    for copy in halos_1:
        copy.wait_recv()
    near(1, (0, 3))
    leaf(1)
    prepare_finish(cur, inverse_diag)
    for copy in reach_1:
        copy.wait_recv()
    coarse(1)
    finish(out, weight)

    for copy in halos + halos_1 + [others, tile_copy, edge] + ring + ring_1 + reach + reach_1:
        copy.wait_send()


def per_device(
    state, near_blocks, basis, leaf_tiles, leaf_links, up_leaf, up_coarse, coarse_tiles, coarse_links,
    down_leaf, diffusion, speed, upwind, zone, rate,
):
    anywhere = pl.BlockSpec(memory_space=pl.ANY)
    vmem = pl.BlockSpec(memory_space=pltpu.VMEM)
    smem = pl.BlockSpec(memory_space=pltpu.SMEM)
    dma = pltpu.SemaphoreType.DMA
    scratch = [
        pltpu.VMEM((4, 128, 256), F32),
        pltpu.VMEM((4, 128, 256), F32),
        pltpu.VMEM((4, 128, 256), F32),
        pltpu.VMEM((4, 128, 256), F32),
        pltpu.VMEM((2, 6, 128, 256), BF16),
        pltpu.VMEM((4, 128, 256), BF16),
        pltpu.VMEM((2, 4, RANK, 64), F32),
        pltpu.VMEM((2, 10, RANK, 128), BF16),
        pltpu.VMEM((2, 5, 64, 256), F32),
        pltpu.VMEM((2, 4, 64, 256), F32),
        pltpu.VMEM((2, 4, 64, 256), I32),
        pltpu.VMEM((4, 64, 256), I32),
        pltpu.VMEM((9, 256, 256), BF16),
        pltpu.VMEM((RANK, 256), BF16),
        pltpu.VMEM((40, RANK, RANK), F32),
        pltpu.VMEM((RANK, 40 * RANK), BF16),
        pltpu.VMEM((4, 40, 64), I32),
        pltpu.VMEM((4, 40, 16, 128), BF16),
        pltpu.VMEM((2, 7 * RANK, 512), BF16),
        pltpu.VMEM((4, RANK, RANK, 64), F32),
        pltpu.VMEM((2, RANK, RANK, 128), F32),
        pltpu.VMEM((4, RANK, RANK, 64), F32),
        pltpu.VMEM((2, RANK, RANK, 128), F32),
        pltpu.VMEM((2, 2, RANK, 128), F32),
        pltpu.VMEM((2, RANK, RANK, 64), F32),
        pltpu.VMEM((2, RANK, RANK, 128), F32),
        pltpu.VMEM((3, 4, 2, 24, RANK), F32),
        pltpu.VMEM((2, RANK, 12 * 64), BF16),
        pltpu.VMEM((8, 128), F32),
        pltpu.VMEM((2, RANK, 128), F32),
        pltpu.VMEM((4, RANK, 128), F32),
        pltpu.VMEM((4, RANK, 128), BF16),
        pltpu.VMEM((2, 4, 8, 128), F32),
        pltpu.VMEM((2, 2, 16, 8, 128), F32),
        dma((14,)),
        dma((4, 8)),
        dma((2, 4)),
        dma((2, 4)),
        dma((2, 13)),
        dma((2, 13)),
        dma((2, 4)),
        dma((2, 4)),
        dma((3,)),
        dma((3,)),
    ]
    result = pl.pallas_call(
        kernel,
        out_shape=pltpu.VMEM((4, 128, 256), F32),
        in_specs=[anywhere] * 12 + [vmem, smem, smem],
        out_specs=vmem,
        scratch_shapes=scratch,
        compiler_params=pltpu.CompilerParams(
            collective_id=0, has_side_effects=True, vmem_limit_bytes=56 * 1024 * 1024
        ),
    )(
        state,
        near_blocks,
        basis.T,
        leaf_tiles,
        jnp.transpose(leaf_links, (1, 2, 0)),
        jnp.transpose(up_leaf, (1, 2, 3, 0)),
        jnp.transpose(down_leaf, (1, 2, 3, 0)),
        jnp.transpose(up_coarse, (0, 2, 3, 1)),
        jnp.transpose(coarse_tiles[:, 0], (0, 1, 3, 2)),
        speed,
        upwind,
        zone,
        jnp.transpose(rate, (1, 2, 0)),
        coarse_links,
        diffusion,
    )
    return jnp.transpose(result.reshape(4, 2, PY, 256), (1, 2, 0, 3))


def solution(mesh):
    return jax.shard_map(
        per_device,
        mesh=mesh,
        in_specs=(
            P("species", None, ("cluster", "owner"), None),
            P(),
            P(),
            P(),
            P(None, ("cluster", "owner"), None),
            P(None, "owner", None, None),
            P(),
            P(None, "cluster", None, None, "owner"),
            P(None, "cluster", None),
            P(None, "owner", None, None),
            P("species"),
            P(None, None, ("cluster", "owner"), None),
            P(None, None, ("cluster", "owner"), None),
            P(None, ("cluster", "owner"), None),
            P(),
        ),
        out_specs=P("species", None, ("cluster", "owner"), None),
        check_vma=False,
    )
```

```python
import jax
import jax.numpy as jnp
from jax import lax
from jax.experimental import pallas as pl
from jax.experimental.pallas import tpu as pltpu
from jax.sharding import PartitionSpec as P

F32 = jnp.float32
BF16 = jnp.bfloat16
I32 = jnp.int32
SWEEPS = 2
STEP = 0.1
RANK = 48
PY = 64
HIGHEST = lax.Precision.HIGHEST
NT = (((1,), (1,)), ((), ()))
TN = (((0,), (0,)), ((), ()))
NN = (((1,), (0,)), ((), ()))
FAR = [(dy, dx) for dy in range(-3, 4) for dx in range(-3, 4) if max(abs(dy), abs(dx)) >= 2]
GROUP_OFFSETS = (2, 3, -2, -3)
REACH = [(d, o) for d in (-3, 3, -2, 2, -1, 1) for o in (0, 1)] + [(0, 1)]


def dot(a, b, dims, precision=None):
    return lax.dot_general(a, b, dims, precision=precision, preferred_element_type=F32)


def lanes(shape):
    return lax.broadcasted_iota(I32, shape, len(shape) - 1)


def rows(shape):
    return lax.broadcasted_iota(I32, shape, len(shape) - 2)


def shift_rows_in_lanes(x, dy):
    if dy == 0:
        return x
    near = pltpu.roll(x, (-dy) % 128, 1)
    wrapped = pltpu.roll(x, (64 - dy) % 128, 1)
    at = lanes(x.shape) % 64 + dy
    return jnp.where((at >= 0) & (at < 64), near, wrapped)


def split_dot(a, b, dims, exact):
    whole = b if exact == 0 else a
    high = whole.astype(BF16)
    rest = (whole - high.astype(F32)).astype(BF16)
    if exact == 0:
        return dot(a, high, dims) + dot(a, rest, dims)
    return dot(high, b, dims) + dot(rest, b, dims)


def row_products(total, a, w_ref, at):
    for r in range(RANK):
        total = total + a[r : r + 1, :] * w_ref[at, r]
    return total


def both_products(totals, left, w_ref, at):
    for r in range(RANK):
        w = w_ref[at, r]
        totals = tuple(total + a[r : r + 1, :] * w for total, a in zip(totals, left))
    return totals


def kernel(
    state, near_blocks, basis_t, leaf_tiles, links, up_leaf, down_leaf, up_coarse, tiles, speed, upwind, zone,
    rate, coarse_links, diffusion,
    out,
    s0, cur, tgt, near_acc, low, oth, ctf, ctb, q, spd, upw, zon, nb, bt, lt, ltt, lk, msk, rhs,
    u_raw, u_wide, d_raw, d_wide, ctw, upc, upg, tcx, t2, tab, cfb, expd, fld, p1, r2,
    load_sem, load8_sem, p1_send, p1_recv, r2_send, r2_recv, halo_send, halo_recv, one_send, one_recv,
):
    cluster = lax.axis_index("cluster")
    owner = lax.axis_index("owner")
    species = lax.axis_index("species")
    n_clusters = lax.axis_size("cluster")
    group = cluster // 4
    y0 = cluster % 4
    n_groups = n_clusters // 4
    line = cluster * 2 + owner
    n_line = n_clusters * 2
    right = lax.rem(line + 1, n_line)
    left = lax.rem(line + n_line - 1, n_line)
    right_id = {"cluster": right // 2, "owner": right % 2}
    left_id = {"cluster": left // 2, "owner": left % 2}
    other_id = {"species": 1 - species}

    def ring_id(k):
        return {"cluster": group * 4 + lax.rem(y0 + k, 4)}

    def reach_id(d, o):
        return {"cluster": lax.rem(group + d + n_groups, n_groups) * 4 + y0, "owner": lax.rem(owner + o, 2)}

    r2[:, :, 7:] = jnp.zeros((SWEEPS, 2, 9, 8, 128), F32)
    barrier = pltpu.get_barrier_semaphore()
    partners = [ring_id(k) for k in (1, 2, 3)] + [reach_id(d, o) for d, o in REACH] + [left_id, right_id, other_id]
    for partner in partners:
        pl.semaphore_signal(barrier, inc=1, device_id=partner, device_id_type=pl.DeviceIdType.MESH)

    def load(src, dst, i):
        copy = pltpu.make_async_copy(src, dst, load_sem.at[i])
        copy.start()
        return copy

    state_loads = []
    for s in range(2):
        for px in range(4):
            copy = pltpu.make_async_copy(state.at[s, :, px], s0.at[px, pl.ds(64 * s, 64)], load8_sem.at[0, s * 4 + px])
            copy.start()
            state_loads.append(copy)
    bt_load = load(basis_t, bt, 0)
    u_loads = [load(up_leaf.at[px], u_raw.at[px], 1 + px) for px in range(4)]
    flow_loads = []
    for j, (src, dst) in enumerate(((speed, spd), (upwind, upw))):
        for e in range(2):
            for px in range(4):
                copy = pltpu.make_async_copy(src.at[e, :, px], dst.at[e, px], load8_sem.at[1 + j, e * 4 + px])
                copy.start()
                flow_loads.append(copy)
    def remote(src, dst, send, recv, device_id):
        return pltpu.make_async_remote_copy(
            src_ref=src, dst_ref=dst, send_sem=send, recv_sem=recv,
            device_id=device_id, device_id_type=pl.DeviceIdType.MESH,
        )

    scale_0 = STEP * diffusion[0]
    scale_1 = STEP * diffusion[1]
    scale = jnp.where(lax.broadcasted_iota(I32, (128, 1), 0) < 64, scale_0, scale_1)

    tab[...] = jnp.zeros_like(tab)

    def own_columns(k, src):
        for px in range(4):
            v = src[px].astype(BF16)
            low[k, px + 1] = v
            coeffs = dot(bt[...], v, NT)
            if k == 0:
                ctf[0, px] = coeffs[:, :64]
                ctf[1, px] = coeffs[:, 64:]
            elif px % 2 == 0:
                even = coeffs
            else:
                ctw[0, px // 2] = jnp.concatenate([even[:, :64], coeffs[:, :64]], axis=1)
                ctw[1, px // 2] = jnp.concatenate([even[:, 64:], coeffs[:, 64:]], axis=1)
            ctb[k, px + 3] = coeffs.astype(BF16)

    def halo_copies(k):
        h, g = halo_send, halo_recv
        return [
            remote(low.at[k, 4], low.at[k, 0], h.at[k, 0], g.at[k, 0], right_id),
            remote(low.at[k, 1], low.at[k, 5], h.at[k, 1], g.at[k, 1], left_id),
            remote(ctb.at[k, pl.ds(4, 3)], ctb.at[k, pl.ds(0, 3)], h.at[k, 2], g.at[k, 2], right_id),
            remote(ctb.at[k, pl.ds(3, 3)], ctb.at[k, pl.ds(7, 3)], h.at[k, 3], g.at[k, 3], left_id),
        ]

    def root_tile(totals):
        total = jnp.concatenate(totals, axis=1)
        width = total.shape[1]
        pick_row = rows((8, width)) - 2 * y0
        mine = (pick_row >= 0) & (pick_row < 2) & (lanes((8, width)) // (width // 2) == pick_row)
        padded = jnp.concatenate([total, jnp.zeros((128 - RANK, width), F32)], axis=0)
        return split_dot(jnp.where(mine, 1.0, 0.0).astype(BF16), padded, NT, 0)

    def send_roots(k):
        copies = [remote(p1.at[k, 0], p1.at[k, j], p1_send.at[k, j], p1_recv.at[k, j], ring_id(j)) for j in (2, 1, 3)]
        for copy in copies:
            copy.start()
        return copies

    def send_groups(k, copies):
        for copy in copies:
            copy.wait_recv()
        tile = p1[k, 0]
        for j in (1, 2, 3):
            tile = tile + p1[k, j]
        r2[k, 0, 3] = tile
        sends = [
            remote(r2.at[k, 0, 3], r2.at[k, o, 3 - d], r2_send.at[k, i], r2_recv.at[k, i], reach_id(d, o))
            for i, (d, o) in enumerate(REACH)
        ]
        for copy in sends:
            copy.start()
        return sends

    def near(k, columns):
        for dy in (0, -1, 1):
            wide = jnp.concatenate(
                [jnp.concatenate([low[k, px + dx + 1] for px in columns], axis=0) for dx in (-1, 0, 1)], axis=1
            )
            at = 3 * (dy + 1)
            part = dot(wide, nb[at : at + 3].reshape(768, 256), NN)
            for b, px in enumerate(columns):
                for s in range(2):
                    block = part[128 * b + 64 * s : 128 * b + 64 * s + 64]
                    if dy == 0:
                        near_acc[px, pl.ds(64 * s, 64)] = block
                    else:
                        near_acc[px, pl.ds(64 * s, 64)] += pltpu.roll(block, (-dy) % 64, 0)

    def leaf(k):
        first = 0
        for dy in range(-3, 4):
            mine = [dx for y, dx in FAR if y == dy]
            n = len(mine)
            side = (dy + 3) % 2
            for px in range(4):
                for i, dx in enumerate(mine):
                    coeffs = ctb[k, px + 3 + dx].reshape(3, 16, 128)
                    masked = coeffs * msk[px, first + i][None]
                    rhs[side, pl.ds(i * RANK, RANK), pl.ds(px * 128, 128)] = masked.reshape(RANK, 128)
            part = dot(ltt[:, first * RANK : (first + n) * RANK], rhs[side, : n * RANK, :], NN)
            for px in range(4):
                piece = shift_rows_in_lanes(part[:, px * 128 : px * 128 + 128], dy)
                if first == 0:
                    expd[px] = piece
                else:
                    expd[px] += piece
            first += n

    def prepare_masks():
        def column(px, _):
            both = jnp.concatenate([lk[px].astype(F32)] * 2, axis=1)
            first = 0
            for dy in range(-3, 4):
                n = sum(1 for y, _ in FAR if y == dy)
                turned = shift_rows_in_lanes(both[first : first + n], -dy)
                for i in range(n):
                    msk[px, first + i] = jnp.broadcast_to(turned[i : i + 1], (16, 128)).astype(BF16)
                first += n
            return 0

        lax.fori_loop(0, 4, column, 0)

    def prepare_leaf_tiles():
        first = 0
        for dy in range(-3, 4):
            n = sum(1 for y, _ in FAR if y == dy)
            stacked = lt[first : first + n].reshape(n * RANK, RANK)
            ltt[:, first * RANK : (first + n) * RANK] = jnp.swapaxes(stacked, 0, 1).astype(BF16)
            first += n

    def prepare_coarse():
        lane = lanes((64, 128))
        at_group = group + lane // 8 - 3 + n_groups
        at_y = (lane // 2) % 4
        for i, target in enumerate(((4 * at_group + at_y) % n_clusters, (2 * at_group + at_y // 2) % (n_clusters // 2))):
            pick = jnp.where((rows((64, 128)) == target) & (lane < 56), 1.0, 0.0).astype(BF16)

            for r in range(0, RANK, 8):
                x = upc[i, r : r + 8].reshape(8 * RANK, 64).astype(BF16)
                upg[i, r : r + 8] = dot(x, pick, NN).reshape(8, RANK, 128)
    def prepare_coarse_tiles():
        t2[...] = jnp.zeros_like(t2)
        for l in range(3):
            for k in range(4):
                at = (l * 4 + k) * 64
                whole = tcx[l, k].reshape(RANK, RANK)
                high = whole.astype(BF16)
                t2[0, :, at : at + RANK] = high
                t2[1, :, at : at + RANK] = (whole - high.astype(F32)).astype(BF16)

    def coarse(k):
        zero = jnp.zeros((RANK, 128), F32)
        lane = lanes((1, 128))
        at_d, at_y = lane // 8 - 3, (lane // 2) % 4
        wide_lane = lanes((RANK, 128))
        values = jnp.swapaxes((r2[k, 0] + r2[k, 1]).reshape(128, 128), 0, 1)[:RANK]
        pieces = []
        for l in range(3):
            if l > 0:
                raised = row_products(zero, values, upg, l - 1)
                hop = 2 * l
                sibling = jnp.where((wide_lane // hop) % 2 == 0, pltpu.roll(raised, 128 - hop, 1), pltpu.roll(raised, hop, 1))
                values = raised + sibling
            for i, offset in enumerate(GROUP_OFFSETS):
                if l == 0:
                    hit = at_d * 4 + at_y == y0 + offset
                elif l == 1:
                    hit = (at_d * 2 + at_y // 2 == y0 // 2 + offset) & (at_y % 2 == 0)
                else:
                    hit = (at_d == offset) & (at_y == 0)
                hit = hit & (lane < 56)
                pieces.append(values * jnp.where(hit, coarse_links[l, 0, i].astype(F32), 0.0))
                pieces.append(jnp.zeros((16, 128), F32))
        stacked = jnp.concatenate(pieces, axis=0)
        high = stacked.astype(BF16)
        rest = (stacked - high.astype(F32)).astype(BF16)
        found = dot(t2[0], high, NN) + (dot(t2[0], rest, NN) + dot(t2[1], high, NN))
        spread = jnp.where(rows((128, 256)) % 2 == lanes((128, 256)) // 128, 1.0, 0.0).astype(BF16)
        both = split_dot(found, spread, NN, 1)
        cfb[0] = both[:, :128]
        cfb[1] = both[:, 128:]

    def expand(j, _):
        zero = jnp.zeros((RANK, 128), F32)
        e0, e1 = both_products((zero, zero), (cfb[0], cfb[1]), d_wide, j)
        for i in range(2):
            half = slice(64 * i, 64 * i + 64)
            expanded = jnp.concatenate([e0[:, half], e1[:, half]], axis=1)
            fld[2 * j + i] = (expd[2 * j + i] + expanded).astype(BF16)
        return 0

    def prepare_finish(src, inverse_diag):
        def column(px, _):
            v = src[px]
            near_acc[px] = v + (tgt[px] - v - scale * near_acc[px]) * inverse_diag
            return 0

        lax.fori_loop(0, 4, column, 0)

    def finish(dst, weight):
        lax.fori_loop(0, 2, expand, 0)
        for px in range(4):
            dst[px] = near_acc[px] - weight * dot(fld[px], bt[...], TN)

    def reaction(px, _):
        z = zon[px]
        values = [jnp.tanh(s0[px, :64]), jnp.tanh(s0[px, 64:])]
        there = oth[px].astype(F32)
        values += [jnp.tanh(there[:64]), jnp.tanh(there[64:])]
        for s in range(2):
            total = jnp.zeros((64, 256), F32)
            for t in range(4):
                table = jnp.broadcast_to(tab[4 * s + t : 4 * s + t + 1, :], (64, 128))
                found = [jnp.take_along_axis(table, z[:, h : h + 128], axis=1) for h in (0, 128)]
                total = total + jnp.concatenate(found, axis=1) * values[t]
            tgt[px, pl.ds(64 * s, 64)] = s0[px, pl.ds(64 * s, 64)] + STEP * total
        return 0

    def advection(s, _):
        at = pl.ds(pl.multiple_of(s * 64, 64), 64)
        n = lanes((64, 256))

        def flux_x(px):
            v = low[0, px + 1, at].astype(F32)
            before = low[0, px, at].astype(F32)
            v_left = pltpu.roll(jnp.where(n % 16 == 15, pltpu.roll(before, 256 - 16, 1), v), 1, 1)
            w = q[0, px]
            return v, w * jnp.where(w > 0, v_left, v)

        v, flux = flux_x(0)
        for px in range(4):
            v_next, flux_next = flux_x(px + 1)
            flux_right = pltpu.roll(jnp.where(n % 16 == 0, pltpu.roll(flux_next, 16, 1), flux), 255, 1)
            v_up = pltpu.roll(jnp.where(n >= 240, pltpu.roll(v, 1, 0), v), 16, 1)
            w = q[1, px]
            flux_y = w * jnp.where(w > 0, v_up, v)
            flux_down = pltpu.roll(jnp.where(n < 16, pltpu.roll(flux_y, 63, 0), flux_y), 256 - 16, 1)
            tgt[px, at] += STEP * (flux - flux_right + flux_y - flux_down)
            v, flux = v_next, flux_next
        return 0

    for copy in state_loads:
        copy.wait()
    bt_load.wait()
    own_columns(0, s0)
    for copy in u_loads:
        copy.wait()
    tiles_load = load(tiles, tcx.at[:, :, owner], 5)
    lk_load = load(links, lk, 7)
    upc_load = load(up_coarse, upc, 8)
    lt_load = load(leaf_tiles, lt, 9)
    d_loads = [load(down_leaf.at[px], d_raw.at[px], 10 + px) for px in range(4)]
    zone_loads = []
    for px in range(4):
        copy = pltpu.make_async_copy(zone.at[:, px], zon.at[px], load8_sem.at[3, px])
        copy.start()
        zone_loads.append(copy)
    nb_load = load(near_blocks, nb, 6)


    def roots():
        totals = lax.fori_loop(
            0, 4, lambda px, t: both_products(t, (ctf[0, px], ctf[1, px]), u_raw, px), (jnp.zeros((RANK, 64), F32),) * 2
        )
        return totals

    def wide_roots():
        zero = jnp.zeros((RANK, 128), F32)
        return lax.fori_loop(
            0, 2, lambda j, t: both_products(t, (ctw[0, j], ctw[1, j]), u_wide, j), (zero, zero)
        )

    def pack(raw, wide):
        def pair(j, _):
            for r in range(RANK):
                wide[j, r] = jnp.concatenate([raw[2 * j, r], raw[2 * j + 1, r]], axis=1)
            return 0

        lax.fori_loop(0, 2, pair, 0)

    p1[0, 0] = root_tile(roots())
    pl.semaphore_wait(barrier, len(partners))
    ring = send_roots(0)
    halos = halo_copies(0)
    others = remote(low.at[0, pl.ds(1, 4)], oth, one_send.at[0], one_recv.at[0], other_id)
    for copy in halos:
        copy.start()
    others.start()
    for copy in flow_loads:
        copy.wait()

    def signed(px, _):
        for e in range(2):
            v = spd[e, px]
            q[e, px] = jnp.where(upw[e, px] == 0, v, -v)
        return 0

    lax.fori_loop(0, 4, signed, 0)
    edge = remote(q.at[0, 0], q.at[0, 4], one_send.at[2], one_recv.at[2], left_id)
    edge.start()
    tiles_load.wait()
    tile_copy = remote(tcx.at[:, :, owner], tcx.at[:, :, owner], one_send.at[1], one_recv.at[1], {"owner": 1 - owner})
    tile_copy.start()

    lk_load.wait()
    prepare_masks()
    lt_load.wait()
    prepare_leaf_tiles()
    upc_load.wait()
    prepare_coarse()
    pack(u_raw, u_wide)
    for copy in d_loads:
        copy.wait()
    pack(d_raw, d_wide)
    reach = send_groups(0, ring)

    for s in range(2):
        for t in range(4):
            at = (2 * species + t) % 4
            tab[4 * s + t : 4 * s + t + 1, :16] = rate[2 * species + s, pl.ds(at, 1), :]
    for copy in zone_loads:
        copy.wait()
    others.wait_recv()
    lax.fori_loop(0, 4, reaction, 0)
    for copy in halos:
        copy.wait_recv()
    edge.wait_recv()
    lax.fori_loop(0, 2, advection, 0)
    nb_load.wait()
    near(0, (0, 1, 2, 3))
    eye = rows((256, 256)) == lanes((256, 256))
    diag = jnp.sum(jnp.where(eye, nb[4].astype(F32), 0.0), axis=0, keepdims=True)
    inverse_diag = 1.0 / (1.0 + scale * diag)
    weight = scale * inverse_diag
    leaf(0)
    tile_copy.wait_recv()
    prepare_coarse_tiles()
    prepare_finish(s0, inverse_diag)
    for copy in reach:
        copy.wait_recv()
    coarse(0)
    finish(cur, weight)

    own_columns(1, cur)
    halos_1 = halo_copies(1)
    p1[1, 0] = root_tile(wide_roots())
    ring_1 = send_roots(1)
    for copy in halos_1:
        copy.start()
    near(1, (1, 2))
    reach_1 = send_groups(1, ring_1)
    for copy in halos_1:
        copy.wait_recv()
    near(1, (0, 3))
    leaf(1)
    prepare_finish(cur, inverse_diag)
    for copy in reach_1:
        copy.wait_recv()
    coarse(1)
    finish(out, weight)

    for copy in halos + halos_1 + [others, tile_copy, edge] + ring + ring_1 + reach + reach_1:
        copy.wait_send()


def per_device(
    state, near_blocks, basis, leaf_tiles, leaf_links, up_leaf, up_coarse, coarse_tiles, coarse_links,
    down_leaf, diffusion, speed, upwind, zone, rate,
):
    anywhere = pl.BlockSpec(memory_space=pl.ANY)
    vmem = pl.BlockSpec(memory_space=pltpu.VMEM)
    smem = pl.BlockSpec(memory_space=pltpu.SMEM)
    dma = pltpu.SemaphoreType.DMA
    scratch = [
        pltpu.VMEM((4, 128, 256), F32),
        pltpu.VMEM((4, 128, 256), F32),
        pltpu.VMEM((4, 128, 256), F32),
        pltpu.VMEM((4, 128, 256), F32),
        pltpu.VMEM((2, 6, 128, 256), BF16),
        pltpu.VMEM((4, 128, 256), BF16),
        pltpu.VMEM((2, 4, RANK, 64), F32),
        pltpu.VMEM((2, 10, RANK, 128), BF16),
        pltpu.VMEM((2, 5, 64, 256), F32),
        pltpu.VMEM((2, 4, 64, 256), F32),
        pltpu.VMEM((2, 4, 64, 256), I32),
        pltpu.VMEM((4, 64, 256), I32),
        pltpu.VMEM((9, 256, 256), BF16),
        pltpu.VMEM((RANK, 256), BF16),
        pltpu.VMEM((40, RANK, RANK), F32),
        pltpu.VMEM((RANK, 40 * RANK), BF16),
        pltpu.VMEM((4, 40, 64), I32),
        pltpu.VMEM((4, 40, 16, 128), BF16),
        pltpu.VMEM((2, 7 * RANK, 512), BF16),
        pltpu.VMEM((4, RANK, RANK, 64), F32),
        pltpu.VMEM((2, RANK, RANK, 128), F32),
        pltpu.VMEM((4, RANK, RANK, 64), F32),
        pltpu.VMEM((2, RANK, RANK, 128), F32),
        pltpu.VMEM((2, 2, RANK, 128), F32),
        pltpu.VMEM((2, RANK, RANK, 64), F32),
        pltpu.VMEM((2, RANK, RANK, 128), F32),
        pltpu.VMEM((3, 4, 2, 24, RANK), F32),
        pltpu.VMEM((2, RANK, 12 * 64), BF16),
        pltpu.VMEM((8, 128), F32),
        pltpu.VMEM((2, RANK, 128), F32),
        pltpu.VMEM((4, RANK, 128), F32),
        pltpu.VMEM((4, RANK, 128), BF16),
        pltpu.VMEM((2, 4, 8, 128), F32),
        pltpu.VMEM((2, 2, 16, 8, 128), F32),
        dma((14,)),
        dma((4, 8)),
        dma((2, 4)),
        dma((2, 4)),
        dma((2, 13)),
        dma((2, 13)),
        dma((2, 4)),
        dma((2, 4)),
        dma((3,)),
        dma((3,)),
    ]
    result = pl.pallas_call(
        kernel,
        out_shape=pltpu.VMEM((4, 128, 256), F32),
        in_specs=[anywhere] * 12 + [vmem, smem, smem],
        out_specs=vmem,
        scratch_shapes=scratch,
        compiler_params=pltpu.CompilerParams(
            collective_id=0, has_side_effects=True, vmem_limit_bytes=56 * 1024 * 1024
        ),
    )(
        state,
        near_blocks,
        basis.T,
        leaf_tiles,
        jnp.transpose(leaf_links, (1, 2, 0)),
        jnp.transpose(up_leaf, (1, 2, 3, 0)),
        jnp.transpose(down_leaf, (1, 2, 3, 0)),
        jnp.transpose(up_coarse, (0, 2, 3, 1)),
        jnp.transpose(coarse_tiles[:, 0], (0, 1, 3, 2)),
        speed,
        upwind,
        zone,
        jnp.transpose(rate, (1, 2, 0)),
        coarse_links,
        diffusion,
    )
    return jnp.transpose(result.reshape(4, 2, PY, 256), (1, 2, 0, 3))


def solution(mesh):
    return jax.shard_map(
        per_device,
        mesh=mesh,
        in_specs=(
            P("species", None, ("cluster", "owner"), None),
            P(),
            P(),
            P(),
            P(None, ("cluster", "owner"), None),
            P(None, "owner", None, None),
            P(),
            P(None, "cluster", None, None, "owner"),
            P(None, "cluster", None),
            P(None, "owner", None, None),
            P("species"),
            P(None, None, ("cluster", "owner"), None),
            P(None, None, ("cluster", "owner"), None),
            P(None, ("cluster", "owner"), None),
            P(),
        ),
        out_specs=P("species", None, ("cluster", "owner"), None),
        check_vma=False,
    )
```
